256 devices in a mesh: wave: 64 (over x, z, core), fld: 4 (over y).
Axes of the slice: x: 4, y: 4, z: 8, core: 2. Of those that a mesh axis runs over, the one named last changes fastest.
Arguments:
- spectral: bfloat16 [4, 128, 2, 640, 640], P('fld', None, None, 'wave'), may hold values from -0.4375 to 0.4375
- legendre: bfloat16 [640, 640, 256], P('wave', None, 'fld'), may hold values from -0.25 to 0.25
- wave_of_row: int32 [640], replicated, may hold values from 0 to 639, each once
- row_points: int32 [256], replicated, may hold values from 20 to 5132, as said below
- lat_slot: int32 [256], replicated, may hold values from 0 to 255, each once
- field_slot: int32 [128], replicated, may hold values from 0 to 127, each once
Outputs:
- grid: bfloat16 [4, 128, 256, 5136], P('fld', 'wave')
The draws below stay inside these ranges and needn't reach their ends.
Inputs may be any that keep to these rules, and one draw needn't show every extreme that they name: `wave_of_row`: each wavenumber 0 to 639 is held by exactly one row. `row_points`: window latitude j is a distinct row i of the octahedral grid's northern half, with 4 i + 16 points; the window's rows come in pairs i and (5120) / 4 - i, so that the points of each pair sum to 5152; the pair with i = 1 is always in the window. `lat_slot`: each window latitude fills exactly one slot. `field_slot`: each level-field pair of a group fills exactly one writer slot.
All inputs are finite; a program needn't handle non-finite values.
Results may differ from the reference program's by a relative error of at most 0.0055.
Values may be sent and summed in bfloat16 or wider, within the bound.
A program may use at most 128 MiB of HBM per device.

```python
import math
import jax
import jax.numpy as jnp
from jax import lax

M = 640
LON = 5136
LAT = 256
P_SIZE = 128
GROUPS = 4


def draw_row_points(key, part):
    key = jax.random.fold_in(key, 7)
    total_rows = (LON - 16) // 4
    half_rows = total_rows // 2
    picked = jax.random.permutation(jax.random.fold_in(key, 1), half_rows - 2)[:LAT // 2 - 1] + 2
    lower = jnp.concatenate([jnp.ones((1,), jnp.int32), picked.astype(jnp.int32)])
    chosen = jnp.concatenate([lower, total_rows - lower])
    chosen = jax.random.permutation(jax.random.fold_in(key, 2), chosen)
    return (4 * chosen + 16).astype(jnp.int32)


def levels(rng, dims, cuts, least, largest):
    def one(dim, parts):
        steps = jax.random.uniform(jax.random.fold_in(jax.random.fold_in(rng, 6), dim), (parts,), jnp.float32, least / len(cuts), largest / len(cuts))
        return jnp.repeat(jnp.exp(steps), dims[dim] // parts).reshape((-1,) + (1,) * (len(dims) - dim - 1))

    loudness = one(*cuts[0])
    for cut in cuts[1:]:
        loudness = loudness * one(*cut)
    return loudness


def normal_values(stream_key, dims, deviation, limit, cuts=(), kind=jnp.bfloat16):
    gain = levels(stream_key, dims, cuts, -0.22, 0.18) if cuts else 1.0
    array = jax.random.normal(stream_key, dims, jnp.float32) * deviation * gain
    return jnp.minimum(jnp.maximum(array, -limit), limit).astype(kind)


def setup_inputs(seed: int = 0) -> dict:
    key_of = jax.random.split(jax.random.key(seed), 7)
    return {
        "spectral": normal_values(key_of[0], (GROUPS, P_SIZE, 2, M, M), ((2 * M) ** -0.5), 0.4375, ((0, 4), (3, 64))),
        "legendre": normal_values(key_of[1], (M, M, LAT), M ** -0.5, 0.25, ((0, 64), (2, 4))),
        "wave_of_row": jax.random.permutation(key_of[2], M).astype(jnp.int32),
        "row_points": draw_row_points(jax.random.fold_in(key_of[6], 71), 0),
        "lat_slot": jax.random.permutation(key_of[4], LAT).astype(jnp.int32),
        "field_slot": jax.random.permutation(key_of[5], P_SIZE).astype(jnp.int32),
    }


def twiddle(wave_numbers, points):
    longitudes = jnp.arange(LON, dtype=jnp.int32)
    residue = (wave_numbers[:, None] * longitudes[None, :]) % points
    phases = (2.0 * math.pi) * residue.astype(jnp.float32) / points.astype(jnp.float32)
    weight = jnp.where(wave_numbers == 0, 1.0, 2.0).astype(jnp.float32)[:, None]
    alive_mask = (2 * wave_numbers[:, None] < points) & (longitudes[None, :] < points)
    cosine = jnp.where(alive_mask, weight * jnp.cos(phases), 0.0)
    sine_part = jnp.where(alive_mask, -weight * jnp.sin(phases), 0.0)
    return jnp.stack([cosine, sine_part]).astype(jnp.bfloat16)


def reference(spectral, legendre, wave_of_row, row_points, lat_slot, field_slot):
    degrees = jnp.arange(M, dtype=jnp.int32)

    def by_row(row_index):
        wave_number = wave_of_row[row_index]
        coeffs = lax.dynamic_index_in_dim(spectral, row_index, 3, keepdims=False).astype(jnp.float32)
        coeffs = jnp.where(degrees >= wave_number, coeffs, jnp.float32(0.0))
        values = lax.dynamic_index_in_dim(legendre, row_index, 0, keepdims=False).astype(jnp.float32)
        return jnp.einsum("gpcn,nj->gpcj", coeffs, values).astype(jnp.bfloat16)

    fourier = lax.map(by_row, jnp.arange(M, dtype=jnp.int32))
    fourier = jnp.transpose(fourier, (4, 0, 1, 2, 3))
    fourier = jnp.take(fourier, lat_slot, axis=0)
    fourier = jnp.take(fourier, field_slot, axis=3)
    slot_points = jnp.take(row_points, lat_slot)
    groups = fourier.shape[2]
    fields = fourier.shape[3]

    def by_slot(slot_index):
        coeff_block = lax.dynamic_index_in_dim(fourier, slot_index, 0, keepdims=False)
        left_side = jnp.transpose(coeff_block, (1, 2, 3, 0)).reshape(groups * fields, 2 * M)
        phase_table = twiddle(wave_of_row, slot_points[slot_index]).reshape(2 * M, LON)
        result = jnp.dot(left_side, phase_table, preferred_element_type=jnp.float32)
        return result.astype(jnp.bfloat16).reshape(groups, fields, LON)

    grid_rows = lax.map(by_slot, jnp.arange(lat_slot.shape[0], dtype=jnp.int32))
    return jnp.transpose(grid_rows, (1, 2, 0, 3))
```

```python
import functools
import math

import jax
import jax.numpy as jnp
from jax import lax
from jax.experimental import pallas as pl
from jax.experimental.pallas import tpu as pltpu
from jax.sharding import PartitionSpec as P

LANES = 128
SUBLANES = 8
COARSE = 48


def turn(product, points, inverse):
    residue = product - jnp.round(product * inverse) * points
    x = residue * inverse * (math.pi / 2)
    y = x * x
    s = x * (1.0 + y * (-1.0 / 6 + y * (1.0 / 120 + y * (-1.0 / 5040))))
    c = 1.0 + y * (-0.5 + y * (1.0 / 24 + y * (-1.0 / 720 + y * (1.0 / 40320))))
    for _ in range(2):
        c, s = 1.0 - 2.0 * s * s, 2.0 * s * c
    return c, s


def times(a, b):
    return a[0] * b[0] - a[1] * b[1], a[0] * b[1] + a[1] * b[0]


def powers(base, count):
    one = (jnp.ones_like(base[0]), jnp.zeros_like(base[0]))
    out = [one, base]
    for i in range(2, count):
        out.append(times(out[i // 2], out[i - i // 2]))
    return out[:count]


def dot_nt(a, b):
    return lax.dot_general(a, b, (((1,), (1,)), ((), ())), preferred_element_type=jnp.float32)


def zonal_kernel(
    four_ref, wave_ref, points_ref, slot_ref, out_ref,
    live, npts, inner_c, inner_s, step_c, step_s, outer_c, outer_s, lead_r, lead_i, left, table, rows,
):
    lat = slot_ref.shape[1]
    waves = wave_ref.shape[1]
    tiles = waves // LANES
    lon = out_ref.shape[1]
    blocks = pl.cdiv(lon, LANES)
    bf16, f32 = jnp.bfloat16, jnp.float32

    held = lax.broadcasted_iota(jnp.int32, (lat, lat), 0)
    by_lane = jnp.where(held == slot_ref[...], 1.0, 0.0).astype(bf16)
    eye = jnp.where(held == lax.broadcasted_iota(jnp.int32, (lat, lat), 1), 1.0, 0.0).astype(bf16)
    chosen = dot_nt(eye, by_lane)
    npts[...] = jnp.broadcast_to(
        jnp.sum(chosen * points_ref[...].astype(f32), axis=1, keepdims=True), (lat, LANES)
    )
    chosen = chosen.astype(bf16)
    for part in range(4):
        moved = dot_nt(chosen, four_ref[part])
        for t in range(tiles):
            live[part, t] = moved[:, t * LANES:(t + 1) * LANES]

    def block(i, carry):
        s0 = pl.multiple_of(i * SUBLANES, SUBLANES)
        points = npts[pl.ds(s0, SUBLANES), :]
        inverse = 1.0 / points
        for t in range(tiles):
            m = jnp.broadcast_to(wave_ref[:, t * LANES:(t + 1) * LANES].astype(f32), points.shape)
            weight = jnp.where(2.0 * m < points, jnp.where(m == 0.0, 1.0, 2.0), 0.0)
            for j, (c, s) in enumerate(powers(turn(m, points, inverse), 8)):
                inner_c[t, pl.ds(j * 8, 8), :] = c
                inner_s[t, pl.ds(j * 8, 8), :] = s
            steps = powers(turn(m * 8.0, points, inverse), 9)
            for j, (c, s) in enumerate(steps):
                step_c[t, pl.ds(j * 8, 8), :] = c
                step_s[t, pl.ds(j * 8, 8), :] = s
            for j, (c, s) in enumerate(powers(turn(m * 128.0, points, inverse), 8)):
                outer_c[t, pl.ds(j * 8, 8), :] = c
                outer_s[t, pl.ds(j * 8, 8), :] = s
            far = powers(turn(m * 1024.0, points, inverse), COARSE // 8)
            for p in range(2):
                value = (
                    live[2 * p, t, pl.ds(s0, SUBLANES), :] * weight,
                    live[2 * p + 1, t, pl.ds(s0, SUBLANES), :] * weight,
                )
                value = times(value, steps[8])
                for a, w in enumerate(far):
                    r, im = times(value, w) if a else value
                    row = (p * (COARSE // 8) + a) * 8
                    lead_r[t, pl.ds(row, 8), :] = r
                    lead_i[t, pl.ds(row, 8), :] = im

        def one(l, buf):
            def bcast(ref, t, row):
                return ref[t, pl.ds(row * 8 + l, 8, stride=0), :]

            def spread(ref, t):
                return ref[t, pl.ds(l, 8, stride=8), :]

            for t in range(tiles):
                ic, isn = spread(inner_c, t), spread(inner_s, t)
                cs, ss = [None] * 16, [None] * 16
                cs[8], ss[8] = ic, isn
                for j in range(1, 9):
                    wc, ws = bcast(step_c, t, j), bcast(step_s, t, j)
                    a, b, c, d = ic * wc, isn * ws, isn * wc, ic * ws
                    if j < 8:
                        cs[8 + j], ss[8 + j] = a - b, c + d
                    cs[8 - j], ss[8 - j] = a + b, c - d
                here = pl.ds(t * LANES, LANES)
                there = pl.ds(waves + t * LANES, LANES)
                for q in range(8):
                    table[buf, pl.ds(q * 16, 16), here] = jnp.concatenate(
                        [cs[2 * q], cs[2 * q + 1]], axis=0).astype(bf16)
                    table[buf, pl.ds(q * 16, 16), there] = jnp.concatenate(
                        [ss[2 * q], ss[2 * q + 1]], axis=0).astype(bf16)
                oc, os = spread(outer_c, t), spread(outer_s, t)
                for q in range(COARSE // 8):
                    res, ims = [], []
                    for h in range(2):
                        fr, fi = bcast(lead_r, t, 2 * q + h), bcast(lead_i, t, 2 * q + h)
                        res.append(fr * oc - fi * os)
                        ims.append(-(fr * os) - fi * oc)
                    left[buf, pl.ds(q * 16, 16), here] = jnp.concatenate(res, axis=0).astype(bf16)
                    left[buf, pl.ds(q * 16, 16), there] = jnp.concatenate(ims, axis=0).astype(bf16)
            rows[pl.ds(s0 + l, 2 * COARSE, stride=lat), :] = dot_nt(left[buf], table[buf])

        def pair(h, carry):
            one(2 * h, 0)
            one(2 * h + 1, 1)
            return carry

        return lax.fori_loop(0, SUBLANES // 2, pair, carry)

    lax.fori_loop(0, lat // SUBLANES, block, 0)

    small = eye[:LANES, :LANES]
    lane = lax.broadcasted_iota(jnp.int32, (lat, LANES), 1).astype(f32)

    def turned(p, a):
        start = pl.multiple_of((p * COARSE + a) * lat, lat)
        value = rows[pl.ds(start, lat), :]
        first = jnp.float32(a * LANES) if isinstance(a, int) else (a * LANES).astype(f32)
        value = jnp.where(lane + first < npts[...], value, 0.0).astype(bf16)
        return dot_nt(small, value).astype(bf16)

    for p in range(2):
        def whole(a, carry, p=p):
            out_ref[p, pl.ds(pl.multiple_of(a * LANES, LANES), LANES), :] = turned(p, a)
            return carry

        lax.fori_loop(0, blocks - 1, whole, 0)
        last = (blocks - 1) * LANES
        out_ref[p, last:, :] = turned(p, blocks - 1)[:lon - last]


def zonal(four, wave_of_row, row_points, lat_slot, lon):
    _, waves, lat = four.shape
    tiles = waves // LANES
    f32 = jnp.float32
    vmem = pl.BlockSpec(memory_space=pltpu.VMEM)

    def scratch(count):
        return pltpu.VMEM((tiles, count * 8, LANES), f32)

    return pl.pallas_call(
        zonal_kernel,
        out_shape=jax.ShapeDtypeStruct((2, lon, lat), jnp.bfloat16),
        in_specs=[vmem] * 4,
        out_specs=vmem,
        scratch_shapes=[
            pltpu.VMEM((4, tiles, lat, LANES), f32),
            pltpu.VMEM((lat, LANES), f32),
            scratch(8), scratch(8), scratch(9), scratch(9), scratch(8), scratch(8),
            scratch(2 * COARSE // 8), scratch(2 * COARSE // 8),
            pltpu.VMEM((2, 2 * COARSE, 2 * waves), jnp.bfloat16),
            pltpu.VMEM((2, LANES, 2 * waves), jnp.bfloat16),
            pltpu.VMEM((2 * COARSE * lat, LANES), f32),
        ],
        compiler_params=pltpu.CompilerParams(vmem_limit_bytes=48 * 1024 * 1024),
        cost_estimate=pl.CostEstimate(
            flops=2 * lat * 2 * COARSE * LANES * 2 * waves, bytes_accessed=7 << 20, transcendentals=0
        ),
    )(four, wave_of_row[None], row_points[None], lat_slot[None])


LON = 5136


def local(spectral, legendre, wave_of_row, row_points, lat_slot, field_slot):
    rows_here, degree_count, _ = legendre.shape
    my_waves = lax.dynamic_slice_in_dim(wave_of_row, lax.axis_index("wave") * rows_here, rows_here)
    degrees = jnp.arange(degree_count, dtype=jnp.int32)
    alive_mask = degrees[None, :] >= my_waves[:, None]
    masked = jnp.where(alive_mask[None, None], spectral[0], jnp.zeros((), jnp.bfloat16))
    fourier = jnp.einsum(
        "pcrn,rnj->pcrj",
        masked,
        lax.all_gather(legendre, "fld", axis=2, tiled=True),
        preferred_element_type=jnp.float32,
    ).astype(jnp.bfloat16)
    fourier = jnp.take(fourier, field_slot, axis=0)
    fourier = lax.all_to_all(fourier, "wave", split_axis=0, concat_axis=2, tiled=True)
    fourier = fourier.reshape(4, -1, lat_slot.shape[0])
    grid = zonal(fourier, wave_of_row, row_points, lat_slot, LON)
    return jnp.transpose(grid, (0, 2, 1))[None]


def solution(mesh):
    in_specs = (P("fld", None, None, "wave", None), P("wave", None, "fld"), P(), P(), P(), P())
    out_specs = P("fld", "wave", None, None)
    return jax.shard_map(local, mesh=mesh, in_specs=in_specs, out_specs=out_specs, check_vma=False)
```

```python
import functools
import math

import jax
import jax.numpy as jnp
from jax import lax
from jax.experimental import pallas as pl
from jax.experimental.pallas import tpu as pltpu
from jax.sharding import PartitionSpec as P

LANES = 128
SUBLANES = 8
COARSE = 48


def turn(product, points, inverse):
    residue = product - jnp.round(product * inverse) * points
    x = residue * inverse * (math.pi / 2)
    y = x * x
    s = x * (1.0 + y * (-1.0 / 6 + y * (1.0 / 120 + y * (-1.0 / 5040))))
    c = 1.0 + y * (-0.5 + y * (1.0 / 24 + y * (-1.0 / 720 + y * (1.0 / 40320))))
    for _ in range(2):
        c, s = 1.0 - 2.0 * s * s, 2.0 * s * c
    return c, s


def times(a, b):
    return a[0] * b[0] - a[1] * b[1], a[0] * b[1] + a[1] * b[0]


def powers(base, count):
    one = (jnp.ones_like(base[0]), jnp.zeros_like(base[0]))
    out = [one, base]
    for i in range(2, count):
        out.append(times(out[i // 2], out[i - i // 2]))
    return out[:count]


def dot_nt(a, b):
    return lax.dot_general(a, b, (((1,), (1,)), ((), ())), preferred_element_type=jnp.float32)


def zonal_kernel(
    four_ref, wave_ref, points_ref, slot_ref, out_ref,
    live, npts, place, inner_c, inner_s, step_c, step_s, outer_c, outer_s, lead_r, lead_i, left, table, rows,
):
    lat = slot_ref.shape[1]
    waves = wave_ref.shape[1]
    tiles = waves // LANES
    lon = out_ref.shape[1]
    blocks = pl.cdiv(lon, LANES)
    bf16, f32 = jnp.bfloat16, jnp.float32

    row_i = lax.broadcasted_iota(jnp.int32, (lat, lat), 0)
    eye = jnp.where(row_i == lax.broadcasted_iota(jnp.int32, (lat, lat), 1), 1.0, 0.0)
    count = points_ref[...].astype(f32)
    count_down = jnp.sum(eye * count, axis=1, keepdims=True)
    rank = jnp.sum(jnp.where(count_down < count, 1.0, 0.0), axis=0, keepdims=True)
    order = jnp.where(row_i.astype(f32) == rank, 1.0, 0.0)
    npts[...] = jnp.broadcast_to(jnp.sum(order * count, axis=1, keepdims=True), (lat, LANES))
    order = order.astype(bf16)
    in_slot = jnp.where(row_i == slot_ref[...], 1.0, 0.0).astype(bf16)
    place[...] = jnp.dot(order, in_slot, preferred_element_type=f32).astype(bf16)
    for part in range(4):
        moved = dot_nt(order, four_ref[part])
        for t in range(tiles):
            live[part, t] = moved[:, t * LANES:(t + 1) * LANES]

    def block(i, carry, far_count):
        s0 = pl.multiple_of(i * SUBLANES, SUBLANES)
        points = npts[pl.ds(s0, SUBLANES), :]
        inverse = 1.0 / points
        for t in range(tiles):
            m = jnp.broadcast_to(wave_ref[:, t * LANES:(t + 1) * LANES].astype(f32), points.shape)
            weight = jnp.where(2.0 * m < points, jnp.where(m == 0.0, 1.0, 2.0), 0.0)
            for j, (c, s) in enumerate(powers(turn(m, points, inverse), 8)):
                inner_c[t, pl.ds(j * 8, 8), :] = c
                inner_s[t, pl.ds(j * 8, 8), :] = s
            steps = powers(turn(m * 8.0, points, inverse), 9)
            for j, (c, s) in enumerate(steps):
                step_c[t, pl.ds(j * 8, 8), :] = c
                step_s[t, pl.ds(j * 8, 8), :] = s
            for j, (c, s) in enumerate(powers(turn(m * 128.0, points, inverse), 8)):
                outer_c[t, pl.ds(j * 8, 8), :] = c
                outer_s[t, pl.ds(j * 8, 8), :] = -s
            far = powers(turn(m * 1024.0, points, inverse), far_count)
            for p in range(2):
                value = (
                    live[2 * p, t, pl.ds(s0, SUBLANES), :] * weight,
                    live[2 * p + 1, t, pl.ds(s0, SUBLANES), :] * weight,
                )
                value = times(value, steps[8])
                for a, w in enumerate(far):
                    r, im = times(value, w) if a else value
                    lead_r[t, pl.ds((a * 2 + p) * 8, 8), :] = r
                    lead_i[t, pl.ds((a * 2 + p) * 8, 8), :] = im

        def make(l, buf):
            def bcast(ref, t, row):
                return ref[t, pl.ds(row * 8 + l, 8, stride=0), :]

            def spread(ref, t):
                return ref[t, pl.ds(l, 8, stride=8), :]

            for t in range(tiles):
                ic, isn = spread(inner_c, t), spread(inner_s, t)
                cs, ss = [None] * 16, [None] * 16
                cs[8], ss[8] = ic, isn
                for j in range(1, 9):
                    wc, ws = bcast(step_c, t, j), bcast(step_s, t, j)
                    a, b, c, d = ic * wc, isn * ws, isn * wc, ic * ws
                    if j < 8:
                        cs[8 + j], ss[8 + j] = a - b, c + d
                    cs[8 - j], ss[8 - j] = a + b, c - d
                here = pl.ds(t * LANES, LANES)
                there = pl.ds(waves + t * LANES, LANES)
                for q in range(8):
                    table[buf, pl.ds(q * 16, 16), here] = jnp.concatenate(
                        [cs[2 * q], cs[2 * q + 1]], axis=0).astype(bf16)
                    table[buf, pl.ds(q * 16, 16), there] = jnp.concatenate(
                        [ss[2 * q], ss[2 * q + 1]], axis=0).astype(bf16)
                oc, os = spread(outer_c, t), spread(outer_s, t)
                for q in range(far_count):
                    res, ims = [], []
                    for h in range(2):
                        fr, fi = bcast(lead_r, t, 2 * q + h), bcast(lead_i, t, 2 * q + h)
                        res.append(fr * oc + fi * os)
                        ims.append(fr * os - fi * oc)
                    left[buf, pl.ds(q * 16, 16), here] = jnp.concatenate(res, axis=0).astype(bf16)
                    left[buf, pl.ds(q * 16, 16), there] = jnp.concatenate(ims, axis=0).astype(bf16)

        def multiply(l, buf):
            rows[pl.ds(s0 + l, 16 * far_count, stride=lat), :] = dot_nt(
                left[buf, :16 * far_count], table[buf])

        make(0, 0)
        for l in range(1, SUBLANES):
            make(l, l % 2)
            multiply(l - 1, (l - 1) % 2)
        multiply(SUBLANES - 1, (SUBLANES - 1) % 2)
        return carry

    start = 0
    for far_count in range(2, COARSE // 8 + 1, 2):
        if far_count == COARSE // 8:
            end = lat // SUBLANES
        else:
            fits = jnp.where(count <= far_count * 1024.0, 1.0, 0.0)
            end = jnp.sum(fits).astype(jnp.int32) // SUBLANES
        lax.fori_loop(start, end, functools.partial(block, far_count=far_count), 0)
        start = end

    small = eye[:LANES, :LANES].astype(bf16)
    lane = lax.broadcasted_iota(jnp.int32, (lat, LANES), 1).astype(f32)

    def turned(p, a):
        at = (a // 8) * 16 + p * 8 + a % 8
        value = rows[pl.ds(pl.multiple_of(at * lat, lat), lat), :]
        first = jnp.float32(a * LANES) if isinstance(a, int) else (a * LANES).astype(f32)
        value = jnp.where(lane + first < npts[...], value, 0.0).astype(bf16)
        value = dot_nt(small, value).astype(bf16)
        return jnp.dot(value, place[...], preferred_element_type=f32).astype(bf16)

    for p in range(2):
        def whole(h, carry, p=p):
            for a in (2 * h, 2 * h + 1):
                out_ref[p, pl.ds(pl.multiple_of(a * LANES, LANES), LANES), :] = turned(p, a)
            return carry

        lax.fori_loop(0, (blocks - 1) // 2, whole, 0)
        for a in range((blocks - 1) // 2 * 2, blocks):
            first = a * LANES
            size = min(LANES, lon - first)
            out_ref[p, first:first + size, :] = turned(p, a)[:size]


def zonal(four, wave_of_row, row_points, lat_slot, lon):
    _, waves, lat = four.shape
    tiles = waves // LANES
    f32 = jnp.float32
    vmem = pl.BlockSpec(memory_space=pltpu.VMEM)

    def scratch(count):
        return pltpu.VMEM((tiles, count * 8, LANES), f32)

    return pl.pallas_call(
        zonal_kernel,
        out_shape=jax.ShapeDtypeStruct((2, lon, lat), jnp.bfloat16),
        in_specs=[vmem] * 4,
        out_specs=vmem,
        scratch_shapes=[
            pltpu.VMEM((4, tiles, lat, LANES), f32),
            pltpu.VMEM((lat, LANES), f32),
            pltpu.VMEM((lat, lat), jnp.bfloat16),
            scratch(8), scratch(8), scratch(9), scratch(9), scratch(8), scratch(8),
            scratch(2 * COARSE // 8), scratch(2 * COARSE // 8),
            pltpu.VMEM((2, 2 * COARSE, 2 * waves), jnp.bfloat16),
            pltpu.VMEM((2, LANES, 2 * waves), jnp.bfloat16),
            pltpu.VMEM((2 * COARSE * lat, LANES), f32),
        ],
        compiler_params=pltpu.CompilerParams(vmem_limit_bytes=48 * 1024 * 1024),
        cost_estimate=pl.CostEstimate(
            flops=2 * lat * 2 * COARSE * LANES * 2 * waves, bytes_accessed=7 << 20, transcendentals=0
        ),
    )(four, wave_of_row[None], row_points[None], lat_slot[None])


LON = 5136


def local(spectral, legendre, wave_of_row, row_points, lat_slot, field_slot):
    rows_here, degree_count, _ = legendre.shape
    my_waves = lax.dynamic_slice_in_dim(wave_of_row, lax.axis_index("wave") * rows_here, rows_here)
    degrees = jnp.arange(degree_count, dtype=jnp.int32)
    alive_mask = degrees[None, :] >= my_waves[:, None]
    masked = jnp.where(alive_mask[None, None], spectral[0], jnp.zeros((), jnp.bfloat16))
    fourier = jnp.einsum(
        "pcrn,rnj->pcrj",
        masked,
        lax.all_gather(legendre, "fld", axis=2, tiled=True),
        preferred_element_type=jnp.float32,
    ).astype(jnp.bfloat16)
    fourier = jnp.take(fourier, field_slot, axis=0)
    fourier = lax.all_to_all(fourier, "wave", split_axis=0, concat_axis=2, tiled=True)
    fourier = fourier.reshape(4, -1, lat_slot.shape[0])
    grid = zonal(fourier, wave_of_row, row_points, lat_slot, LON)
    return jnp.transpose(grid, (0, 2, 1))[None]


def solution(mesh):
    in_specs = (P("fld", None, None, "wave", None), P("wave", None, "fld"), P(), P(), P(), P())
    out_specs = P("fld", "wave", None, None)
    return jax.shard_map(local, mesh=mesh, in_specs=in_specs, out_specs=out_specs, check_vma=False)
```

```python
import functools
import math

import jax
import jax.numpy as jnp
from jax import lax
from jax.experimental import pallas as pl
from jax.experimental.pallas import tpu as pltpu
from jax.sharding import PartitionSpec as P

LANES = 128
SUBLANES = 8
MESSAGE = 16
COARSE = 48


def turn(product, points, inverse):
    residue = product - jnp.round(product * inverse) * points
    x = residue * inverse * (math.pi / 2)
    y = x * x
    s = x * (1.0 + y * (-1.0 / 6 + y * (1.0 / 120 + y * (-1.0 / 5040))))
    c = 1.0 + y * (-0.5 + y * (1.0 / 24 + y * (-1.0 / 720 + y * (1.0 / 40320))))
    for _ in range(2):
        c, s = 1.0 - 2.0 * s * s, 2.0 * s * c
    return c, s


def times(a, b):
    return a[0] * b[0] - a[1] * b[1], a[0] * b[1] + a[1] * b[0]


def powers(base, count):
    one = (jnp.ones_like(base[0]), jnp.zeros_like(base[0]))
    out = [one, base]
    for i in range(2, count):
        out.append(times(out[i // 2], out[i - i // 2]))
    return out[:count]


def dot_nt(a, b):
    return lax.dot_general(a, b, (((1,), (1,)), ((), ())), preferred_element_type=jnp.float32)


def zonal_kernel(
    four_ref, wave_ref, points_ref, slot_ref, out_ref,
    live, npts, place, wide, held, inner_c, inner_s, step_c, step_s, outer_c, outer_s, lead_r, lead_i, left, table, rows,
):
    lat = slot_ref.shape[1]
    waves = wave_ref.shape[1]
    tiles = waves // LANES
    lon = out_ref.shape[1]
    blocks = pl.cdiv(lon, LANES)
    bf16, f32 = jnp.bfloat16, jnp.float32

    row_i = lax.broadcasted_iota(jnp.int32, (lat, lat), 0)
    eye = jnp.where(row_i == lax.broadcasted_iota(jnp.int32, (lat, lat), 1), 1.0, 0.0)
    count = points_ref[...].astype(f32)
    count_down = jnp.sum(eye * count, axis=1, keepdims=True)
    rank = jnp.sum(jnp.where(count_down < count, 1.0, 0.0), axis=0, keepdims=True)
    order = jnp.where(row_i.astype(f32) == rank, 1.0, 0.0)
    npts[...] = jnp.broadcast_to(jnp.sum(order * count, axis=1, keepdims=True), (lat, LANES))
    order = order.astype(bf16)
    in_slot = jnp.where(row_i == slot_ref[...], 1.0, 0.0).astype(bf16)
    place[...] = jnp.dot(order, in_slot, preferred_element_type=f32).astype(bf16)
    sources = four_ref.shape[1] // MESSAGE
    for chunk in range(four_ref.shape[0]):
        wide[...] = four_ref[chunk].astype(f32)
        for part in range(4):
            for r in range(2):
                halves = [wide[pl.ds(part * 4 + r * 2 + h, sources, stride=MESSAGE), :] for h in range(2)]
                held[part, pl.ds((chunk * 2 + r) * sources, sources), :] = jnp.concatenate(
                    halves, axis=1).astype(bf16)
    for part in range(4):
        moved = dot_nt(order, held[part])
        for t in range(tiles):
            live[part, t] = moved[:, t * LANES:(t + 1) * LANES]

    def block(i, carry, far_count):
        s0 = pl.multiple_of(i * SUBLANES, SUBLANES)
        points = npts[pl.ds(s0, SUBLANES), :]
        inverse = 1.0 / points
        for t in range(tiles):
            m = jnp.broadcast_to(wave_ref[:, t * LANES:(t + 1) * LANES].astype(f32), points.shape)
            weight = jnp.where(2.0 * m < points, jnp.where(m == 0.0, 1.0, 2.0), 0.0)
            half = turn(m, 2.0 * points, 0.5 * inverse)
            steps = powers(turn(m * 8.0, points, inverse), 5)
            for j, (c, s) in enumerate(steps):
                step_c[t, pl.ds(j * 8, 8), :] = c
                step_s[t, pl.ds(j * 8, 8), :] = s
            middle = times(half, steps[4])
            for j, w in enumerate(powers(times(half, half), 8)):
                c, s = times(middle, w) if j else middle
                inner_c[t, pl.ds(j * 8, 8), :] = c
                inner_s[t, pl.ds(j * 8, 8), :] = s
            centre = times(times(steps[4], steps[4]), (half[0], -half[1]))
            for j, (c, s) in enumerate(powers(turn(m * 128.0, points, inverse), 8)):
                outer_c[t, pl.ds(j * 8, 8), :] = c
                outer_s[t, pl.ds(j * 8, 8), :] = s
            far = powers(turn(m * 1024.0, points, inverse), far_count)
            for p in range(2):
                value = (
                    live[2 * p, t, pl.ds(s0, SUBLANES), :] * weight,
                    live[2 * p + 1, t, pl.ds(s0, SUBLANES), :] * weight,
                )
                value = times(value, centre)
                for a, w in enumerate(far):
                    r, im = times(value, w) if a else value
                    lead_r[t, pl.ds((a * 2 + p) * 8, 8), :] = r
                    lead_i[t, pl.ds((a * 2 + p) * 8, 8), :] = im

        def make(l, buf):
            def bcast(ref, t, row):
                return ref[t, pl.ds(row * 8 + l, 8, stride=0), :]

            def spread(ref, t):
                return ref[t, pl.ds(l, 8, stride=8), :]

            for t in range(tiles):
                ic, isn = spread(inner_c, t), spread(inner_s, t)
                cs, ss = [None] * 8, [None] * 8
                cs[4], ss[4] = ic, isn
                for j in range(1, 5):
                    wc, ws = bcast(step_c, t, j), bcast(step_s, t, j)
                    a, b, c, d = ic * wc, isn * ws, isn * wc, ic * ws
                    if j < 4:
                        cs[4 + j], ss[4 + j] = a - b, c + d
                    cs[4 - j], ss[4 - j] = a + b, c - d
                here = pl.ds(t * LANES, LANES)
                there = pl.ds(waves + t * LANES, LANES)
                for q in range(4):
                    table[buf, pl.ds(q * 16, 16), here] = jnp.concatenate(
                        [cs[2 * q], cs[2 * q + 1]], axis=0).astype(bf16)
                    table[buf, pl.ds(q * 16, 16), there] = jnp.concatenate(
                        [ss[2 * q], ss[2 * q + 1]], axis=0).astype(bf16)
                oc, os = spread(outer_c, t), spread(outer_s, t)
                for q in range(far_count):
                    res, ims = [], []
                    for h in range(2):
                        fr, fi = bcast(lead_r, t, 2 * q + h), bcast(lead_i, t, 2 * q + h)
                        res.append(fr * oc - fi * os)
                        ims.append(fr * os + fi * oc)
                    left[buf, pl.ds(q * 16, 16), here] = jnp.concatenate(res, axis=0).astype(bf16)
                    left[buf, pl.ds(q * 16, 16), there] = jnp.concatenate(ims, axis=0).astype(bf16)

        def multiply(l, buf):
            used = pl.ds(0, 16 * far_count)
            even = dot_nt(left[buf, used, :waves], table[buf, :, :waves])
            odd = dot_nt(left[buf, used, waves:], table[buf, :, waves:])
            rows[pl.ds(s0 + l, 16 * far_count, stride=lat), :] = jnp.concatenate(
                [even - odd, even + odd], axis=1)

        make(0, 0)
        for l in range(1, SUBLANES):
            make(l, l % 2)
            multiply(l - 1, (l - 1) % 2)
        multiply(SUBLANES - 1, (SUBLANES - 1) % 2)
        return carry

    start = 0
    for far_count in range(2, COARSE // 8 + 1, 2):
        if far_count == COARSE // 8:
            end = lat // SUBLANES
        else:
            fits = jnp.where(count <= far_count * 1024.0, 1.0, 0.0)
            end = jnp.sum(fits).astype(jnp.int32) // SUBLANES
        lax.fori_loop(start, end, functools.partial(block, far_count=far_count), 0)
        start = end

    def longitude_of(shape):
        lane = lax.broadcasted_iota(jnp.int32, shape, 1)
        return jnp.where(lane < LANES // 2, lane + LANES // 2, LANES - 1 - lane)

    square = (LANES, LANES)
    small = jnp.where(lax.broadcasted_iota(jnp.int32, square, 0) == longitude_of(square), 1.0, 0.0).astype(bf16)
    lane = longitude_of((lat, LANES)).astype(f32)

    def turned(p, a):
        at = (a // 8) * 16 + p * 8 + a % 8
        value = rows[pl.ds(pl.multiple_of(at * lat, lat), lat), :]
        first = jnp.float32(a * LANES) if isinstance(a, int) else (a * LANES).astype(f32)
        value = jnp.where(lane + first < npts[...], value, 0.0).astype(bf16)
        value = dot_nt(small, value).astype(bf16)
        return jnp.dot(value, place[...], preferred_element_type=f32).astype(bf16)

    for p in range(2):
        def whole(h, carry, p=p):
            for a in (2 * h, 2 * h + 1):
                out_ref[p, pl.ds(pl.multiple_of(a * LANES, LANES), LANES), :] = turned(p, a)
            return carry

        lax.fori_loop(0, (blocks - 1) // 2, whole, 0)
        for a in range((blocks - 1) // 2 * 2, blocks):
            first = a * LANES
            size = min(LANES, lon - first)
            out_ref[p, first:first + size, :] = turned(p, a)[:size]


def zonal(four, wave_of_row, row_points, lat_slot, lon):
    waves, lat = wave_of_row.shape[0], lat_slot.shape[0]
    tiles = waves // LANES
    f32 = jnp.float32
    vmem = pl.BlockSpec(memory_space=pltpu.VMEM)

    def scratch(count):
        return pltpu.VMEM((tiles, count * 8, LANES), f32)

    return pl.pallas_call(
        zonal_kernel,
        out_shape=jax.ShapeDtypeStruct((2, lon, lat), jnp.bfloat16),
        in_specs=[vmem] * 4,
        out_specs=vmem,
        scratch_shapes=[
            pltpu.VMEM((4, tiles, lat, LANES), f32),
            pltpu.VMEM((lat, LANES), f32),
            pltpu.VMEM((lat, lat), jnp.bfloat16),
            pltpu.VMEM(four.shape[1:], f32),
            pltpu.VMEM((4, waves, lat), jnp.bfloat16),
            scratch(8), scratch(8), scratch(5), scratch(5), scratch(8), scratch(8),
            scratch(2 * COARSE // 8), scratch(2 * COARSE // 8),
            pltpu.VMEM((2, 2 * COARSE, 2 * waves), jnp.bfloat16),
            pltpu.VMEM((2, LANES // 2, 2 * waves), jnp.bfloat16),
            pltpu.VMEM((2 * COARSE * lat, LANES), f32),
        ],
        compiler_params=pltpu.CompilerParams(vmem_limit_bytes=48 * 1024 * 1024),
        cost_estimate=pl.CostEstimate(
            flops=2 * lat * 2 * COARSE * LANES * 2 * waves, bytes_accessed=7 << 20, transcendentals=0
        ),
    )(four, wave_of_row[None], row_points[None], lat_slot[None])


LON = 5136
MESH = pl.DeviceIdType.MESH


def spectral_kernel(
    spec_ref, leg_ref, wave_ref, field_ref, recv_ref,
    legs, swap, mixed, outbox,
    own_sem, send_a, recv_a, send_f, recv_f, send_m, recv_m, keep_m,
):
    bf16, f32 = jnp.bfloat16, jnp.float32
    me, y = lax.axis_index("wave"), lax.axis_index("fld")
    peers, ring = lax.axis_size("wave"), lax.axis_size("fld")
    right, left = lax.rem(y + 1, ring), lax.rem(y + ring - 1, ring)
    rows_here, lats_here, degrees = leg_ref.shape
    chunks = rows_here // 2
    pairs = spec_ref.shape[1]

    def there(k):
        return lax.rem(me + k, peers)

    barrier = pltpu.get_barrier_semaphore()

    def greet(k, carry):
        pl.semaphore_signal(barrier, inc=1, device_id=(there(k), y), device_id_type=MESH)
        return carry

    for side in (right, left):
        pl.semaphore_signal(barrier, inc=1, device_id=(me, side), device_id_type=MESH)
    lax.fori_loop(1, peers, greet, 0)

    def own():
        return pltpu.make_async_copy(leg_ref, legs.at[y], own_sem)

    def first(c, side):
        at = pl.ds(2 * c, 2)
        return pltpu.make_async_remote_copy(
            src_ref=leg_ref.at[at], dst_ref=legs.at[y, at],
            send_sem=send_a.at[side, c], recv_sem=recv_a.at[side, c],
            device_id=(me, (right, left)[side]), device_id_type=MESH)

    def second(c, side):
        block, at = (left, right)[side], pl.ds(2 * c + side, 1)
        return pltpu.make_async_remote_copy(
            src_ref=legs.at[block, at], dst_ref=legs.at[block, at],
            send_sem=send_f.at[side, c], recv_sem=recv_f.at[side, c],
            device_id=(me, (right, left)[side]), device_id_type=MESH)

    def message(c, k):
        return pltpu.make_async_remote_copy(
            src_ref=outbox.at[c, there(k)], dst_ref=recv_ref.at[c, me],
            send_sem=send_m.at[c], recv_sem=recv_m.at[c],
            device_id=(there(k), y), device_id_type=MESH)

    def all_messages(c):
        some = pl.ds(0, peers - 1)
        return pltpu.make_async_remote_copy(
            src_ref=outbox.at[c, some], dst_ref=recv_ref.at[c, some],
            send_sem=send_m.at[c], recv_sem=recv_m.at[c],
            device_id=(there(1), y), device_id_type=MESH)

    def kept(c):
        return pltpu.make_async_copy(outbox.at[c, me], recv_ref.at[c, me], keep_m.at[c])

    own().start()

    row_i = lax.broadcasted_iota(jnp.int32, (pairs, pairs), 0)
    col_i = lax.broadcasted_iota(jnp.int32, (pairs, pairs), 1)
    eye = jnp.where(row_i == col_i, 1.0, 0.0).astype(bf16)
    twice_i = lax.broadcasted_iota(jnp.int32, (pairs // 2, pairs), 1)
    twice = jnp.where(
        lax.broadcasted_iota(jnp.int32, (pairs // 2, pairs), 0) == twice_i // 2, 1.0, 0.0).astype(bf16)
    fields = jnp.broadcast_to(field_ref[...].astype(f32), (8, pairs // 2)).astype(bf16)
    wanted = 2.0 * jnp.dot(fields, twice, preferred_element_type=f32)[0:1]
    wanted = wanted + (col_i[0:1] % 2).astype(f32)
    swap[...] = dot_nt(eye, jnp.where(row_i.astype(f32) == wanted, 1.0, 0.0).astype(bf16)).astype(bf16)

    own().wait()
    pl.semaphore_wait(barrier, peers + 1)
    for c in range(3):
        for side in range(2):
            first(c, side).start()

    def pass_on(c):
        for side in range(2):
            first(c, side).wait_recv()
        for side in range(2):
            second(c, side).start()

    pass_on(0)

    def step(c, carry):
        @pl.when(c < chunks - 1)
        def _():
            pass_on(c + 1)

        @pl.when(c < chunks - 3)
        def _():
            for side in range(2):
                first(c + 3, side).start()

        for side in range(2):
            second(c, side).wait_recv()
        degree = lax.broadcasted_iota(jnp.int32, (ring * lats_here, degrees), 1)
        for r in range(2):
            row = 2 * c + r
            values = jnp.concatenate([legs[g, row] for g in range(ring)], axis=0)
            values = jnp.where(degree >= wave_ref[me * rows_here + row], values.astype(f32), 0.0).astype(bf16)
            fourier = dot_nt(spec_ref[row], values).astype(bf16)
            fourier = jnp.dot(swap[...], fourier, preferred_element_type=f32)
            for h in range(2):
                mixed[pl.ds(r * 2 + h, pairs, stride=4), :] = fourier[:, h * LANES:(h + 1) * LANES]
        outbox[c] = mixed[...].astype(bf16).reshape(outbox.shape[1:])
        kept(c).start()

        def post(k, carry):
            message(c, k).start()
            return carry

        return lax.fori_loop(1, peers, post, carry)

    lax.fori_loop(0, chunks, step, 0)

    def finish(c, carry):
        for side in range(2):
            first(c, side).wait_send()
            second(c, side).wait_send()
        kept(c).wait()
        all_messages(c).wait()
        return carry

    lax.fori_loop(0, chunks, finish, 0)


def spectral_part(spec, legendre, wave_of_row, field_slot, peers, ring):
    rows_here, pairs, degrees = spec.shape
    lats_here = legendre.shape[1]
    chunks = rows_here // 2
    bf16 = jnp.bfloat16
    vmem = pl.BlockSpec(memory_space=pltpu.VMEM)
    pairs_sem = pltpu.SemaphoreType.DMA((2, chunks))
    chunk_sem = pltpu.SemaphoreType.DMA((chunks,))
    return pl.pallas_call(
        spectral_kernel,
        out_shape=jax.ShapeDtypeStruct((chunks, peers, MESSAGE, LANES), bf16),
        in_specs=[vmem, vmem, pl.BlockSpec(memory_space=pltpu.SMEM), vmem],
        out_specs=pl.BlockSpec(memory_space=pl.ANY),
        scratch_shapes=[
            pltpu.VMEM((ring, rows_here, lats_here, degrees), bf16),
            pltpu.VMEM((pairs, pairs), bf16),
            pltpu.VMEM((peers * MESSAGE, LANES), jnp.float32),
            pltpu.VMEM((chunks, peers, MESSAGE, LANES), bf16),
            pltpu.SemaphoreType.DMA,
            pairs_sem, pairs_sem, pairs_sem, pairs_sem, chunk_sem, chunk_sem, chunk_sem,
        ],
        compiler_params=pltpu.CompilerParams(
            collective_id=0, has_side_effects=True, vmem_limit_bytes=40 * 1024 * 1024),
        cost_estimate=pl.CostEstimate(
            flops=2 * rows_here * pairs * degrees * lats_here * ring, bytes_accessed=6 << 20, transcendentals=0),
    )(spec, legendre, wave_of_row, field_slot[None])


def local(spectral, legendre, wave_of_row, row_points, lat_slot, field_slot):
    rows_here, degree_count, _ = legendre.shape
    peers, ring = lax.axis_size("wave"), lax.axis_size("fld")
    spec = jnp.transpose(spectral[0], (2, 0, 1, 3)).reshape(rows_here, -1, degree_count)
    four = spectral_part(spec, jnp.transpose(legendre, (0, 2, 1)), wave_of_row, field_slot, peers, ring)
    four = four.reshape(rows_here // 2, peers * MESSAGE, LANES)
    waves = wave_of_row.reshape(peers, rows_here).T.reshape(-1)
    grid = zonal(four, waves, row_points, lat_slot, LON)
    return jnp.transpose(grid, (0, 2, 1))[None]


def solution(mesh):
    in_specs = (P("fld", None, None, "wave", None), P("wave", None, "fld"), P(), P(), P(), P())
    out_specs = P("fld", "wave", None, None)
    return jax.shard_map(local, mesh=mesh, in_specs=in_specs, out_specs=out_specs, check_vma=False)
```

```python
import functools
import math

import jax
import jax.numpy as jnp
from jax import lax
from jax.experimental import pallas as pl
from jax.experimental.pallas import tpu as pltpu
from jax.sharding import PartitionSpec as P

LANES = 128
SUBLANES = 8
MESSAGE = 16
COARSE = 48


def turn(product, points, inverse):
    residue = product - jnp.round(product * inverse) * points
    x = residue * inverse * (math.pi / 2)
    y = x * x
    s = x * (1.0 + y * (-1.0 / 6 + y * (1.0 / 120 + y * (-1.0 / 5040))))
    c = 1.0 + y * (-0.5 + y * (1.0 / 24 + y * (-1.0 / 720 + y * (1.0 / 40320))))
    for _ in range(2):
        c, s = 1.0 - 2.0 * s * s, 2.0 * s * c
    return c, s


def times(a, b):
    return a[0] * b[0] - a[1] * b[1], a[0] * b[1] + a[1] * b[0]


def powers(base, count):
    one = (jnp.ones_like(base[0]), jnp.zeros_like(base[0]))
    out = [one, base]
    for i in range(2, count):
        out.append(times(out[i // 2], out[i - i // 2]))
    return out[:count]


def dot_nt(a, b):
    return lax.dot_general(a, b, (((1,), (1,)), ((), ())), preferred_element_type=jnp.float32)


def zonal_kernel(
    four_ref, wave_ref, points_ref, slot_ref, out_ref,
    live, npts, place, wide, held, inner_c, inner_s, step_c, step_s, outer_c, outer_s, lead_r, lead_i, left, table, rows,
):
    lat = slot_ref.shape[1]
    waves = wave_ref.shape[1]
    tiles = waves // LANES
    lon = out_ref.shape[1]
    blocks = pl.cdiv(lon, LANES)
    bf16, f32 = jnp.bfloat16, jnp.float32

    row_i = lax.broadcasted_iota(jnp.int32, (lat, lat), 0)
    eye = jnp.where(row_i == lax.broadcasted_iota(jnp.int32, (lat, lat), 1), 1.0, 0.0)
    count = points_ref[...].astype(f32)
    count_down = jnp.sum(eye * count, axis=1, keepdims=True)
    rank = jnp.sum(jnp.where(count_down < count, 1.0, 0.0), axis=0, keepdims=True)
    order = jnp.where(row_i.astype(f32) == rank, 1.0, 0.0)
    npts[...] = jnp.broadcast_to(jnp.sum(order * count, axis=1, keepdims=True), (lat, LANES))
    order = order.astype(bf16)
    in_slot = jnp.where(row_i == slot_ref[...], 1.0, 0.0).astype(bf16)
    place[...] = jnp.dot(order, in_slot, preferred_element_type=f32).astype(bf16)
    sources = four_ref.shape[1] // MESSAGE
    for chunk in range(four_ref.shape[0]):
        wide[...] = four_ref[chunk].astype(f32)
        for part in range(4):
            for r in range(2):
                halves = [wide[pl.ds(part * 4 + r * 2 + h, sources, stride=MESSAGE), :] for h in range(2)]
                held[part, pl.ds((chunk * 2 + r) * sources, sources), :] = jnp.concatenate(
                    halves, axis=1).astype(bf16)
    for part in range(4):
        moved = dot_nt(order, held[part])
        for t in range(tiles):
            live[part, t] = moved[:, t * LANES:(t + 1) * LANES]

    def block(i, carry, far_count):
        s0 = pl.multiple_of(i * SUBLANES, SUBLANES)
        points = npts[pl.ds(s0, SUBLANES), :]
        inverse = 1.0 / points
        for t in range(tiles):
            m = jnp.broadcast_to(wave_ref[:, t * LANES:(t + 1) * LANES].astype(f32), points.shape)
            weight = jnp.where(2.0 * m < points, jnp.where(m == 0.0, 1.0, 2.0), 0.0)
            half = turn(m, 2.0 * points, 0.5 * inverse)
            near = powers(times(half, half), 9)
            steps = powers(near[8], 5)
            for j, (c, s) in enumerate(steps):
                step_c[t, pl.ds(j * 8, 8), :] = c
                step_s[t, pl.ds(j * 8, 8), :] = s
            middle = times(half, steps[4])
            for j, w in enumerate(near[:8]):
                c, s = times(middle, w) if j else middle
                inner_c[t, pl.ds(j * 8, 8), :] = c
                inner_s[t, pl.ds(j * 8, 8), :] = s
            centre = times(times(steps[4], steps[4]), (half[0], -half[1]))
            outer = powers(turn(m * 128.0, points, inverse), 9)
            for j, (c, s) in enumerate(outer[:8]):
                outer_c[t, pl.ds(j * 8, 8), :] = c
                outer_s[t, pl.ds(j * 8, 8), :] = s
            far = powers(outer[8], far_count)
            for p in range(2):
                value = (
                    live[2 * p, t, pl.ds(s0, SUBLANES), :] * weight,
                    live[2 * p + 1, t, pl.ds(s0, SUBLANES), :] * weight,
                )
                value = times(value, centre)
                for a, w in enumerate(far):
                    r, im = times(value, w) if a else value
                    lead_r[t, pl.ds((a * 2 + p) * 8, 8), :] = r
                    lead_i[t, pl.ds((a * 2 + p) * 8, 8), :] = im

        def make(l, buf):
            def bcast(ref, t, row):
                return ref[t, pl.ds(row * 8 + l, 8, stride=0), :]

            def spread(ref, t):
                return ref[t, pl.ds(l, 8, stride=8), :]

            for t in range(tiles):
                ic, isn = spread(inner_c, t), spread(inner_s, t)
                cs, ss = [None] * 8, [None] * 8
                cs[4], ss[4] = ic, isn
                for j in range(1, 5):
                    wc, ws = bcast(step_c, t, j), bcast(step_s, t, j)
                    a, b, c, d = ic * wc, isn * ws, isn * wc, ic * ws
                    if j < 4:
                        cs[4 + j], ss[4 + j] = a - b, c + d
                    cs[4 - j], ss[4 - j] = a + b, c - d
                here = pl.ds(t * LANES, LANES)
                there = pl.ds(waves + t * LANES, LANES)
                for q in range(4):
                    table[buf, pl.ds(q * 16, 16), here] = jnp.concatenate(
                        [cs[2 * q], cs[2 * q + 1]], axis=0).astype(bf16)
                    table[buf, pl.ds(q * 16, 16), there] = jnp.concatenate(
                        [ss[2 * q], ss[2 * q + 1]], axis=0).astype(bf16)
                oc, os = spread(outer_c, t), spread(outer_s, t)
                for q in range(far_count):
                    res, ims = [], []
                    for h in range(2):
                        fr, fi = bcast(lead_r, t, 2 * q + h), bcast(lead_i, t, 2 * q + h)
                        res.append(fr * oc - fi * os)
                        ims.append(fr * os + fi * oc)
                    left[buf, pl.ds(q * 16, 16), here] = jnp.concatenate(res, axis=0).astype(bf16)
                    left[buf, pl.ds(q * 16, 16), there] = jnp.concatenate(ims, axis=0).astype(bf16)

        def multiply(l, buf):
            used = pl.ds(0, 16 * far_count)
            even = dot_nt(left[buf, used, :waves], table[buf, :, :waves])
            odd = dot_nt(left[buf, used, waves:], table[buf, :, waves:])
            rows[pl.ds(s0 + l, 16 * far_count, stride=lat), :] = jnp.concatenate(
                [even - odd, even + odd], axis=1)

        make(0, 0)
        for l in range(1, SUBLANES):
            make(l, l % 2)
            multiply(l - 1, (l - 1) % 2)
        multiply(SUBLANES - 1, (SUBLANES - 1) % 2)
        return carry

    start = 0
    for far_count in range(2, COARSE // 8 + 1, 2):
        if far_count == COARSE // 8:
            end = lat // SUBLANES
        else:
            fits = jnp.where(count <= far_count * 1024.0, 1.0, 0.0)
            end = jnp.sum(fits).astype(jnp.int32) // SUBLANES
        lax.fori_loop(start, end, functools.partial(block, far_count=far_count), 0)
        start = end

    def longitude_of(shape):
        lane = lax.broadcasted_iota(jnp.int32, shape, 1)
        return jnp.where(lane < LANES // 2, lane + LANES // 2, LANES - 1 - lane)

    square = (LANES, LANES)
    small = jnp.where(lax.broadcasted_iota(jnp.int32, square, 0) == longitude_of(square), 1.0, 0.0).astype(bf16)
    lane = longitude_of((lat, LANES)).astype(f32)

    def turned(p, a):
        at = (a // 8) * 16 + p * 8 + a % 8
        value = rows[pl.ds(pl.multiple_of(at * lat, lat), lat), :]
        first = jnp.float32(a * LANES) if isinstance(a, int) else (a * LANES).astype(f32)
        value = jnp.where(lane + first < npts[...], value, 0.0).astype(bf16)
        value = dot_nt(small, value).astype(bf16)
        return jnp.dot(value, place[...], preferred_element_type=f32).astype(bf16)

    for p in range(2):
        def whole(h, carry, p=p):
            for a in (2 * h, 2 * h + 1):
                out_ref[p, pl.ds(pl.multiple_of(a * LANES, LANES), LANES), :] = turned(p, a)
            return carry

        lax.fori_loop(0, (blocks - 1) // 2, whole, 0)
        for a in range((blocks - 1) // 2 * 2, blocks):
            first = a * LANES
            size = min(LANES, lon - first)
            out_ref[p, first:first + size, :] = turned(p, a)[:size]


def zonal(four, wave_of_row, row_points, lat_slot, lon):
    waves, lat = wave_of_row.shape[0], lat_slot.shape[0]
    tiles = waves // LANES
    f32 = jnp.float32
    vmem = pl.BlockSpec(memory_space=pltpu.VMEM)

    def scratch(count):
        return pltpu.VMEM((tiles, count * 8, LANES), f32)

    return pl.pallas_call(
        zonal_kernel,
        out_shape=jax.ShapeDtypeStruct((2, lon, lat), jnp.bfloat16),
        in_specs=[vmem] * 4,
        out_specs=vmem,
        scratch_shapes=[
            pltpu.VMEM((4, tiles, lat, LANES), f32),
            pltpu.VMEM((lat, LANES), f32),
            pltpu.VMEM((lat, lat), jnp.bfloat16),
            pltpu.VMEM(four.shape[1:], f32),
            pltpu.VMEM((4, waves, lat), jnp.bfloat16),
            scratch(8), scratch(8), scratch(5), scratch(5), scratch(8), scratch(8),
            scratch(2 * COARSE // 8), scratch(2 * COARSE // 8),
            pltpu.VMEM((2, 2 * COARSE, 2 * waves), jnp.bfloat16),
            pltpu.VMEM((2, LANES // 2, 2 * waves), jnp.bfloat16),
            pltpu.VMEM((2 * COARSE * lat, LANES), f32),
        ],
        compiler_params=pltpu.CompilerParams(vmem_limit_bytes=48 * 1024 * 1024),
        cost_estimate=pl.CostEstimate(
            flops=2 * lat * 2 * COARSE * LANES * 2 * waves, bytes_accessed=7 << 20, transcendentals=0
        ),
    )(four, wave_of_row[None], row_points[None], lat_slot[None])


LON = 5136
MESH = pl.DeviceIdType.MESH


def spectral_kernel(
    spec_ref, leg_ref, wave_ref, field_ref, recv_ref,
    legs, swap, lefts, mixed, outbox,
    own_sem, send_a, recv_a, send_f, recv_f, send_m, recv_m, keep_m,
):
    bf16, f32 = jnp.bfloat16, jnp.float32
    me, y = lax.axis_index("wave"), lax.axis_index("fld")
    peers, ring = lax.axis_size("wave"), lax.axis_size("fld")
    right, left = lax.rem(y + 1, ring), lax.rem(y + ring - 1, ring)
    rows_here, lats_here, degrees = leg_ref.shape
    chunks = rows_here // 2
    pairs = spec_ref.shape[0] * spec_ref.shape[2]

    def there(k):
        other = me + k
        return jnp.where(other >= peers, other - peers, other)

    barrier = pltpu.get_barrier_semaphore()

    def greet(k, carry):
        pl.semaphore_signal(barrier, inc=1, device_id=(there(k), y), device_id_type=MESH)
        return carry

    for side in (right, left):
        pl.semaphore_signal(barrier, inc=1, device_id=(me, side), device_id_type=MESH)
    lax.fori_loop(1, peers, greet, 0, unroll=9)

    def own():
        return pltpu.make_async_copy(leg_ref, legs.at[y], own_sem)

    def first(c, side):
        at = pl.ds(2 * c, 2)
        return pltpu.make_async_remote_copy(
            src_ref=leg_ref.at[at], dst_ref=legs.at[y, at],
            send_sem=send_a.at[side, c], recv_sem=recv_a.at[side, c],
            device_id=(me, (right, left)[side]), device_id_type=MESH)

    def second(c, side):
        block, at = (left, right)[side], pl.ds(2 * c + side, 1)
        return pltpu.make_async_remote_copy(
            src_ref=legs.at[block, at], dst_ref=legs.at[block, at],
            send_sem=send_f.at[side, c], recv_sem=recv_f.at[side, c],
            device_id=(me, (right, left)[side]), device_id_type=MESH)

    def message(c, k):
        other = there(k)
        return pltpu.make_async_remote_copy(
            src_ref=outbox.at[c, other], dst_ref=recv_ref.at[c, me],
            send_sem=send_m.at[c], recv_sem=recv_m.at[c],
            device_id=(other, y), device_id_type=MESH)

    def all_messages(c):
        some = pl.ds(0, peers - 1)
        return pltpu.make_async_remote_copy(
            src_ref=outbox.at[c, some], dst_ref=recv_ref.at[c, some],
            send_sem=send_m.at[c], recv_sem=recv_m.at[c],
            device_id=(there(1), y), device_id_type=MESH)

    def kept(c):
        return pltpu.make_async_copy(outbox.at[c, me], recv_ref.at[c, me], keep_m.at[c])

    own().start()

    row_i = lax.broadcasted_iota(jnp.int32, (pairs, pairs), 0)
    col_i = lax.broadcasted_iota(jnp.int32, (pairs, pairs), 1)
    eye = jnp.where(row_i == col_i, 1.0, 0.0).astype(bf16)
    twice_i = lax.broadcasted_iota(jnp.int32, (pairs // 2, pairs), 1)
    twice = jnp.where(
        lax.broadcasted_iota(jnp.int32, (pairs // 2, pairs), 0) == twice_i // 2, 1.0, 0.0).astype(bf16)
    fields = jnp.broadcast_to(field_ref[...].astype(f32), (8, pairs // 2)).astype(bf16)
    wanted = 2.0 * jnp.dot(fields, twice, preferred_element_type=f32)[0:1]
    wanted = wanted + (col_i[0:1] % 2).astype(f32)
    swap[...] = dot_nt(eye, jnp.where(row_i.astype(f32) == wanted, 1.0, 0.0).astype(bf16)).astype(bf16)

    own().wait()
    pl.semaphore_wait(barrier, peers + 1)
    for c in range(2):
        for side in range(2):
            first(c, side).start()

    def pass_on(c):
        for side in range(2):
            first(c, side).wait_recv()
        for side in range(2):
            second(c, side).start()

        @pl.when(c < chunks - 2)
        def _():
            for side in range(2):
                first(c + 2, side).start()

    pass_on(0)

    def step(c, carry):
        @pl.when(c < chunks - 1)
        def _():
            pass_on(c + 1)

        for r in range(2):
            lefts[r] = spec_ref[:, 2 * c + r].reshape(pairs, degrees)
        for side in range(2):
            second(c, side).wait_recv()
        degree = lax.broadcasted_iota(jnp.int32, (ring * lats_here, degrees), 1)
        for r in range(2):
            row = 2 * c + r
            values = jnp.concatenate([legs[g, row] for g in range(ring)], axis=0)
            values = jnp.where(degree >= wave_ref[me * rows_here + row], values.astype(f32), 0.0).astype(bf16)
            fourier = dot_nt(lefts[r], values).astype(bf16)
            fourier = jnp.dot(swap[...], fourier, preferred_element_type=f32)
            for h in range(2):
                mixed[pl.ds(r * 2 + h, pairs, stride=4), :] = fourier[:, h * LANES:(h + 1) * LANES]
        outbox[c] = mixed[...].astype(bf16).reshape(outbox.shape[1:])
        kept(c).start()

        def post(k, carry):
            message(c, k).start()
            return carry

        return lax.fori_loop(1, peers, post, carry, unroll=9)

    lax.fori_loop(0, chunks, step, 0)

    def finish(c, carry):
        for side in range(2):
            first(c, side).wait_send()
            second(c, side).wait_send()
        kept(c).wait()
        all_messages(c).wait()
        return carry

    lax.fori_loop(0, chunks, finish, 0)


def spectral_part(spec, legendre, wave_of_row, field_slot, peers, ring):
    pairs, degrees = spec.shape[0] * spec.shape[2], spec.shape[3]
    rows_here = spec.shape[1]
    lats_here = legendre.shape[1]
    chunks = rows_here // 2
    bf16 = jnp.bfloat16
    vmem = pl.BlockSpec(memory_space=pltpu.VMEM)
    pairs_sem = pltpu.SemaphoreType.DMA((2, chunks))
    chunk_sem = pltpu.SemaphoreType.DMA((chunks,))
    return pl.pallas_call(
        spectral_kernel,
        out_shape=jax.ShapeDtypeStruct((chunks, peers, MESSAGE, LANES), bf16),
        in_specs=[vmem, vmem, pl.BlockSpec(memory_space=pltpu.SMEM), vmem],
        out_specs=pl.BlockSpec(memory_space=pl.ANY),
        scratch_shapes=[
            pltpu.VMEM((ring, rows_here, lats_here, degrees), bf16),
            pltpu.VMEM((pairs, pairs), bf16),
            pltpu.VMEM((2, pairs, degrees), bf16),
            pltpu.VMEM((peers * MESSAGE, LANES), jnp.float32),
            pltpu.VMEM((chunks, peers, MESSAGE, LANES), bf16),
            pltpu.SemaphoreType.DMA,
            pairs_sem, pairs_sem, pairs_sem, pairs_sem, chunk_sem, chunk_sem, chunk_sem,
        ],
        compiler_params=pltpu.CompilerParams(
            collective_id=0, has_side_effects=True, vmem_limit_bytes=40 * 1024 * 1024),
        cost_estimate=pl.CostEstimate(
            flops=2 * rows_here * pairs * degrees * lats_here * ring, bytes_accessed=6 << 20, transcendentals=0),
    )(spec, legendre, wave_of_row, field_slot[None])


def local(spectral, legendre, wave_of_row, row_points, lat_slot, field_slot):
    rows_here, degree_count, _ = legendre.shape
    peers, ring = lax.axis_size("wave"), lax.axis_size("fld")
    spec = jnp.transpose(spectral[0], (0, 2, 1, 3))
    four = spectral_part(spec, jnp.transpose(legendre, (0, 2, 1)), wave_of_row, field_slot, peers, ring)
    four = four.reshape(rows_here // 2, peers * MESSAGE, LANES)
    waves = wave_of_row.reshape(peers, rows_here).T.reshape(-1)
    grid = zonal(four, waves, row_points, lat_slot, LON)
    return jnp.transpose(grid, (0, 2, 1))[None]


def solution(mesh):
    in_specs = (P("fld", None, None, "wave", None), P("wave", None, "fld"), P(), P(), P(), P())
    out_specs = P("fld", "wave", None, None)
    return jax.shard_map(local, mesh=mesh, in_specs=in_specs, out_specs=out_specs, check_vma=False)
```

```python
import functools
import math

import jax
import jax.numpy as jnp
from jax import lax
from jax.experimental import pallas as pl
from jax.experimental.pallas import tpu as pltpu
from jax.sharding import PartitionSpec as P

LANES = 128
SUBLANES = 8
TOGETHER = 2
MESSAGE = 16
BUNDLES = ((0, 2), (2, 2), (4, 1))
COARSE = 48


def turn(product, points, inverse):
    residue = product - jnp.round(product * inverse) * points
    x = residue * inverse * (math.pi / 2)
    y = x * x
    s = x * (1.0 + y * (-1.0 / 6 + y * (1.0 / 120 + y * (-1.0 / 5040))))
    c = 1.0 + y * (-0.5 + y * (1.0 / 24 + y * (-1.0 / 720 + y * (1.0 / 40320))))
    for _ in range(2):
        c, s = 1.0 - 2.0 * s * s, 2.0 * s * c
    return c, s


def times(a, b):
    return a[0] * b[0] - a[1] * b[1], a[0] * b[1] + a[1] * b[0]


def powers(base, count):
    one = (jnp.ones_like(base[0]), jnp.zeros_like(base[0]))
    out = [one, base]
    for i in range(2, count):
        out.append(times(out[i // 2], out[i - i // 2]))
    return out[:count]


def dot_nt(a, b):
    return lax.dot_general(a, b, (((1,), (1,)), ((), ())), preferred_element_type=jnp.float32)


def zonal_kernel(
    four_ref, wave_ref, points_ref, slot_ref, out_ref,
    live, npts, place, wide, held, inner_c, inner_s, step_c, step_s, outer_c, outer_s, leap_c, leap_s, lead_r, lead_i, left, table, rows,
):
    lat = slot_ref.shape[1]
    waves = wave_ref.shape[1]
    tiles = waves // LANES
    lon = out_ref.shape[1]
    blocks = pl.cdiv(lon, LANES)
    bf16, f32 = jnp.bfloat16, jnp.float32

    row_i = lax.broadcasted_iota(jnp.int32, (lat, lat), 0)
    eye = jnp.where(row_i == lax.broadcasted_iota(jnp.int32, (lat, lat), 1), 1.0, 0.0)
    count = points_ref[...].astype(f32)
    count_down = jnp.sum(eye * count, axis=1, keepdims=True)
    rank = jnp.sum(jnp.where(count_down < count, 1.0, 0.0), axis=0, keepdims=True)
    order = jnp.where(row_i.astype(f32) == rank, 1.0, 0.0)
    npts[...] = jnp.broadcast_to(jnp.sum(order * count, axis=1, keepdims=True), (lat, LANES))
    order = order.astype(bf16)
    in_slot = jnp.where(row_i == slot_ref[...], 1.0, 0.0).astype(bf16)
    place[...] = jnp.dot(order, in_slot, preferred_element_type=f32).astype(bf16)
    sources = four_ref.shape[0]
    for chunk in range(four_ref.shape[1] // MESSAGE):
        wide[...] = four_ref[:, pl.ds(chunk * MESSAGE, MESSAGE), :].astype(f32).reshape(wide.shape)
        for part in range(4):
            for r in range(2):
                halves = [wide[pl.ds(part * 4 + r * 2 + h, sources, stride=MESSAGE), :] for h in range(2)]
                held[part, pl.ds((chunk * 2 + r) * sources, sources), :] = jnp.concatenate(
                    halves, axis=1).astype(bf16)
    for part in range(4):
        moved = dot_nt(order, held[part])
        for t in range(tiles):
            live[part, t] = moved[:, t * LANES:(t + 1) * LANES]

    groups = SUBLANES // TOGETHER

    def multiply(t0, buf, far_count):
        count = 16 * far_count
        used, half = pl.ds(0, TOGETHER * count), LANES // 2
        even = dot_nt(left[buf, used, :waves], table[buf, :, :waves])
        odd = dot_nt(left[buf, used, waves:], table[buf, :, waves:])
        for l in range(TOGETHER):
            e = even[l * count:(l + 1) * count, l * half:(l + 1) * half]
            o = odd[l * count:(l + 1) * count, l * half:(l + 1) * half]
            rows[pl.ds(t0 + l, count, stride=lat), :] = jnp.concatenate([e - o, e + o], axis=1)

    def block(i, carry, far_count, first):
        middle_step = far_count // 2 - 1
        s0 = pl.multiple_of(i * SUBLANES, SUBLANES)
        points = npts[pl.ds(s0, SUBLANES), :]
        inverse = 1.0 / points
        for t in range(tiles):
            m = jnp.broadcast_to(wave_ref[:, t * LANES:(t + 1) * LANES].astype(f32), points.shape)
            weight = jnp.where(2.0 * m < points, jnp.where(m == 0.0, 1.0, 2.0), 0.0)
            half = turn(m, 2.0 * points, 0.5 * inverse)
            near = powers(times(half, half), 9)
            steps = powers(near[8], 5)
            for j, (c, s) in enumerate(steps):
                step_c[t, pl.ds(j * 8, 8), :] = c
                step_s[t, pl.ds(j * 8, 8), :] = s
            middle = times(half, steps[4])
            for j, w in enumerate(near[:8]):
                c, s = times(middle, w) if j else middle
                inner_c[t, pl.ds(j * 8, 8), :] = c
                inner_s[t, pl.ds(j * 8, 8), :] = s
            centre = times(times(steps[4], steps[4]), (half[0], -half[1]))
            outer = powers(turn(m * 128.0, points, inverse), 9)
            for j, (c, s) in enumerate(outer[:8]):
                outer_c[t, pl.ds(j * 8, 8), :] = c
                outer_s[t, pl.ds(j * 8, 8), :] = s
            far = powers(outer[8], far_count - middle_step)
            for j, (c, s) in enumerate(far[1:]):
                leap_c[t, pl.ds(j * 8, 8), :] = c
                leap_s[t, pl.ds(j * 8, 8), :] = s
            if middle_step:
                centre = times(centre, far[middle_step])
            for p in range(2):
                value = (
                    live[2 * p, t, pl.ds(s0, SUBLANES), :] * weight,
                    live[2 * p + 1, t, pl.ds(s0, SUBLANES), :] * weight,
                )
                r, im = times(value, centre)
                lead_r[t, pl.ds(p * 8, 8), :] = r
                lead_i[t, pl.ds(p * 8, 8), :] = im

        def make(l, buf):
            low, high = l % TOGETHER * (LANES // 2), l % TOGETHER * 16 * far_count

            def bcast(ref, t, row):
                return ref[t, pl.ds(row * 8 + l, 8, stride=0), :]

            def spread(ref, t):
                return ref[t, pl.ds(l, 8, stride=8), :]

            for t in range(tiles):
                ic, isn = spread(inner_c, t), spread(inner_s, t)
                cs, ss = [None] * 8, [None] * 8
                cs[4], ss[4] = ic, isn
                for j in range(1, 5):
                    wc, ws = bcast(step_c, t, j), bcast(step_s, t, j)
                    a, b, c, d = ic * wc, isn * ws, isn * wc, ic * ws
                    if j < 4:
                        cs[4 + j], ss[4 + j] = a - b, c + d
                    cs[4 - j], ss[4 - j] = a + b, c - d
                here = pl.ds(t * LANES, LANES)
                there = pl.ds(waves + t * LANES, LANES)
                for q in range(4):
                    table[buf, pl.ds(low + q * 16, 16), here] = jnp.concatenate(
                        [cs[2 * q], cs[2 * q + 1]], axis=0).astype(bf16)
                    table[buf, pl.ds(low + q * 16, 16), there] = jnp.concatenate(
                        [ss[2 * q], ss[2 * q + 1]], axis=0).astype(bf16)
                oc, os = spread(outer_c, t), spread(outer_s, t)
                parts = [[None] * far_count for _ in range(2)]
                for p in range(2):
                    parts[p][middle_step] = times(
                        (bcast(lead_r, t, p), bcast(lead_i, t, p)), (oc, os))
                for j in range(1, far_count - middle_step):
                    wc, ws = bcast(leap_c, t, j - 1), bcast(leap_s, t, j - 1)
                    for p in range(2):
                        r, im = parts[p][middle_step]
                        a, b, c, d = r * wc, im * ws, im * wc, r * ws
                        parts[p][middle_step + j] = (a - b, c + d)
                        if j <= middle_step:
                            parts[p][middle_step - j] = (a + b, c - d)
                for q in range(far_count):
                    for i, where in enumerate((here, there)):
                        left[buf, pl.ds(high + q * 16, 16), where] = jnp.concatenate(
                            [parts[0][q][i], parts[1][q][i]], axis=0).astype(bf16)

        for g in range(groups):
            for l in range(g * TOGETHER, (g + 1) * TOGETHER):
                make(l, g % 2)
            if g:
                multiply(s0 + (g - 1) * TOGETHER, (g - 1) % 2, far_count)
            else:
                before = jnp.where(i > first, s0 - TOGETHER, s0 + SUBLANES - TOGETHER)
                multiply(before, (groups - 1) % 2, far_count)
        return carry

    start = 0
    for far_count in range(2, COARSE // 8 + 1, 2):
        if far_count == COARSE // 8:
            end = lat // SUBLANES
        else:
            fits = jnp.where(count <= far_count * 1024.0, 1.0, 0.0)
            end = jnp.sum(fits).astype(jnp.int32) // SUBLANES
        lax.fori_loop(start, end, functools.partial(block, far_count=far_count, first=start), 0)

        @pl.when(end > start)
        def _(end=end, far_count=far_count):
            multiply(end * SUBLANES - TOGETHER, (groups - 1) % 2, far_count)

        start = end

    def longitude_of(shape):
        lane = lax.broadcasted_iota(jnp.int32, shape, 1)
        return jnp.where(lane < LANES // 2, lane + LANES // 2, LANES - 1 - lane)

    square = (LANES, LANES)
    small = jnp.where(lax.broadcasted_iota(jnp.int32, square, 0) == longitude_of(square), 1.0, 0.0).astype(bf16)
    lane = longitude_of((lat, LANES)).astype(f32)

    def turned(p, a):
        at = (a // 8) * 16 + p * 8 + a % 8
        value = rows[pl.ds(pl.multiple_of(at * lat, lat), lat), :]
        first = jnp.float32(a * LANES) if isinstance(a, int) else (a * LANES).astype(f32)
        value = jnp.where(lane + first < npts[...], value, 0.0).astype(bf16)
        value = dot_nt(small, value).astype(bf16)
        return jnp.dot(value, place[...], preferred_element_type=f32).astype(bf16)

    for p in range(2):
        def whole(h, carry, p=p):
            for a in (2 * h, 2 * h + 1):
                out_ref[p, pl.ds(pl.multiple_of(a * LANES, LANES), LANES), :] = turned(p, a)
            return carry

        lax.fori_loop(0, (blocks - 1) // 2, whole, 0)
        for a in range((blocks - 1) // 2 * 2, blocks):
            first = a * LANES
            size = min(LANES, lon - first)
            out_ref[p, first:first + size, :] = turned(p, a)[:size]


def zonal(four, wave_of_row, row_points, lat_slot, lon):
    waves, lat = wave_of_row.shape[0], lat_slot.shape[0]
    tiles = waves // LANES
    f32 = jnp.float32
    vmem = pl.BlockSpec(memory_space=pltpu.VMEM)

    def scratch(count):
        return pltpu.VMEM((tiles, count * 8, LANES), f32)

    return pl.pallas_call(
        zonal_kernel,
        out_shape=jax.ShapeDtypeStruct((2, lon, lat), jnp.bfloat16),
        in_specs=[vmem] * 4,
        out_specs=vmem,
        scratch_shapes=[
            pltpu.VMEM((4, tiles, lat, LANES), f32),
            pltpu.VMEM((lat, LANES), f32),
            pltpu.VMEM((lat, lat), jnp.bfloat16),
            pltpu.VMEM((four.shape[0] * MESSAGE, LANES), f32),
            pltpu.VMEM((4, waves, lat), jnp.bfloat16),
            scratch(8), scratch(8), scratch(5), scratch(5), scratch(8), scratch(8),
            scratch(COARSE // 16), scratch(COARSE // 16), scratch(2), scratch(2),
            pltpu.VMEM((2, TOGETHER * 2 * COARSE, 2 * waves), jnp.bfloat16),
            pltpu.VMEM((2, TOGETHER * LANES // 2, 2 * waves), jnp.bfloat16),
            pltpu.VMEM((2 * COARSE * lat, LANES), f32),
        ],
        compiler_params=pltpu.CompilerParams(vmem_limit_bytes=48 * 1024 * 1024),
        cost_estimate=pl.CostEstimate(
            flops=2 * lat * 2 * COARSE * LANES * 2 * waves, bytes_accessed=7 << 20, transcendentals=0
        ),
    )(four, wave_of_row[None], row_points[None], lat_slot[None])


LON = 5136
MESH = pl.DeviceIdType.MESH


def spectral_kernel(
    spec_hbm, leg_ref, wave_ref, field_ref, recv_ref,
    spec_ref, legs, swap, lefts, mixed, outbox,
    spec_sem, own_sem, send_a, recv_a, send_f, recv_f, send_m, recv_m, keep_m,
):
    bf16, f32 = jnp.bfloat16, jnp.float32
    me, y = lax.axis_index("wave"), lax.axis_index("fld")
    peers, ring = lax.axis_size("wave"), lax.axis_size("fld")
    right, left = lax.rem(y + 1, ring), lax.rem(y + ring - 1, ring)
    rows_here, lats_here, degrees = leg_ref.shape
    chunks = rows_here // 2
    pairs = spec_ref.shape[0] * spec_ref.shape[2]

    def there(k):
        other = me + k
        return jnp.where(other >= peers, other - peers, other)

    barrier = pltpu.get_barrier_semaphore()

    def greet(k, carry):
        pl.semaphore_signal(barrier, inc=1, device_id=(there(k), y), device_id_type=MESH)
        return carry

    for side in (right, left):
        pl.semaphore_signal(barrier, inc=1, device_id=(me, side), device_id_type=MESH)
    lax.fori_loop(1, peers, greet, 0, unroll=9)

    def own():
        return pltpu.make_async_copy(leg_ref, legs.at[y], own_sem)

    def first(c, side):
        at = pl.ds(2 * c, 2)
        return pltpu.make_async_remote_copy(
            src_ref=leg_ref.at[at], dst_ref=legs.at[y, at],
            send_sem=send_a.at[side, c], recv_sem=recv_a.at[side, c],
            device_id=(me, (right, left)[side]), device_id_type=MESH)

    def second(c, side):
        block, at = (left, right)[side], pl.ds(2 * c + side, 1)
        return pltpu.make_async_remote_copy(
            src_ref=legs.at[block, at], dst_ref=legs.at[block, at],
            send_sem=send_f.at[side, c], recv_sem=recv_f.at[side, c],
            device_id=(me, (right, left)[side]), device_id_type=MESH)

    def rows_of(g):
        return pl.ds(BUNDLES[g][0] * MESSAGE, BUNDLES[g][1] * MESSAGE)

    def message(g, k):
        other = there(k)
        return pltpu.make_async_remote_copy(
            src_ref=outbox.at[other, rows_of(g)], dst_ref=recv_ref.at[me, rows_of(g)],
            send_sem=send_m.at[g], recv_sem=recv_m.at[g],
            device_id=(other, y), device_id_type=MESH)

    def all_messages(g):
        some = pl.ds(0, peers - 1)
        return pltpu.make_async_remote_copy(
            src_ref=outbox.at[some, rows_of(g)], dst_ref=recv_ref.at[some, rows_of(g)],
            send_sem=send_m.at[g], recv_sem=recv_m.at[g],
            device_id=(there(1), y), device_id_type=MESH)

    def kept(g):
        return pltpu.make_async_copy(outbox.at[me, rows_of(g)], recv_ref.at[me, rows_of(g)], keep_m.at[g])

    def spec_copy():
        return pltpu.make_async_copy(spec_hbm, spec_ref, spec_sem)

    spec_copy().start()
    own().start()

    row_i = lax.broadcasted_iota(jnp.int32, (pairs, pairs), 0)
    col_i = lax.broadcasted_iota(jnp.int32, (pairs, pairs), 1)
    eye = jnp.where(row_i == col_i, 1.0, 0.0).astype(bf16)
    twice_i = lax.broadcasted_iota(jnp.int32, (pairs // 2, pairs), 1)
    twice = jnp.where(
        lax.broadcasted_iota(jnp.int32, (pairs // 2, pairs), 0) == twice_i // 2, 1.0, 0.0).astype(bf16)
    fields = jnp.broadcast_to(field_ref[...].astype(f32), (8, pairs // 2)).astype(bf16)
    wanted = 2.0 * jnp.dot(fields, twice, preferred_element_type=f32)[0:1]
    wanted = wanted + (col_i[0:1] % 2).astype(f32)
    swap[...] = dot_nt(eye, jnp.where(row_i.astype(f32) == wanted, 1.0, 0.0).astype(bf16)).astype(bf16)

    own().wait()
    pl.semaphore_wait(barrier, peers + 1)
    for c in range(2):
        for side in range(2):
            first(c, side).start()
    spec_copy().wait()

    def pass_on(c):
        for side in range(2):
            first(c, side).wait_recv()
        for side in range(2):
            second(c, side).start()

        @pl.when(c < chunks - 2)
        def _():
            for side in range(2):
                first(c + 2, side).start()

    pass_on(0)

    def step(c, carry):
        @pl.when(c < chunks - 1)
        def _():
            pass_on(c + 1)

        for r in range(2):
            lefts[r] = spec_ref[:, 2 * c + r].reshape(pairs, degrees)
        for side in range(2):
            second(c, side).wait_recv()
        degree = lax.broadcasted_iota(jnp.int32, (ring * lats_here, degrees), 1)
        for r in range(2):
            row = 2 * c + r
            values = jnp.concatenate([legs[g, row] for g in range(ring)], axis=0)
            values = jnp.where(degree >= wave_ref[me * rows_here + row], values.astype(f32), 0.0).astype(bf16)
            fourier = dot_nt(lefts[r], values).astype(bf16)
            fourier = jnp.dot(swap[...], fourier, preferred_element_type=f32)
            for h in range(2):
                mixed[pl.ds(r * 2 + h, pairs, stride=4), :] = fourier[:, h * LANES:(h + 1) * LANES]
        outbox[:, pl.ds(pl.multiple_of(c * MESSAGE, MESSAGE), MESSAGE), :] = mixed[...].astype(bf16).reshape(
            peers, MESSAGE, LANES)
        return carry

    for g, (c0, size) in enumerate(BUNDLES):
        lax.fori_loop(c0, c0 + size, step, 0)
        kept(g).start()

        def post(k, carry, g=g):
            message(g, k).start()
            return carry

        lax.fori_loop(1, peers, post, 0, unroll=9)

    def finish(c, carry):
        for side in range(2):
            first(c, side).wait_send()
            second(c, side).wait_send()
        return carry

    lax.fori_loop(0, chunks, finish, 0)
    for g in range(len(BUNDLES)):
        kept(g).wait()
        all_messages(g).wait()


def spectral_part(spec, legendre, wave_of_row, field_slot, peers, ring):
    pairs, degrees = spec.shape[0] * spec.shape[2], spec.shape[3]
    rows_here = spec.shape[1]
    lats_here = legendre.shape[1]
    chunks = rows_here // 2
    bf16 = jnp.bfloat16
    vmem = pl.BlockSpec(memory_space=pltpu.VMEM)
    hbm = pl.BlockSpec(memory_space=pltpu.HBM)
    pairs_sem = pltpu.SemaphoreType.DMA((2, chunks))
    bundle_sem = pltpu.SemaphoreType.DMA((len(BUNDLES),))
    return pl.pallas_call(
        spectral_kernel,
        out_shape=jax.ShapeDtypeStruct((peers, chunks * MESSAGE, LANES), bf16),
        in_specs=[hbm, hbm, pl.BlockSpec(memory_space=pltpu.SMEM), vmem],
        out_specs=pl.BlockSpec(memory_space=pl.ANY),
        scratch_shapes=[
            pltpu.VMEM(spec.shape, bf16),
            pltpu.VMEM((ring, rows_here, lats_here, degrees), bf16),
            pltpu.VMEM((pairs, pairs), bf16),
            pltpu.VMEM((2, pairs, degrees), bf16),
            pltpu.VMEM((peers * MESSAGE, LANES), jnp.float32),
            pltpu.VMEM((peers, chunks * MESSAGE, LANES), bf16),
            pltpu.SemaphoreType.DMA,
            pltpu.SemaphoreType.DMA,
            pairs_sem, pairs_sem, pairs_sem, pairs_sem, bundle_sem, bundle_sem, bundle_sem,
        ],
        compiler_params=pltpu.CompilerParams(
            collective_id=0, has_side_effects=True, vmem_limit_bytes=40 * 1024 * 1024),
        cost_estimate=pl.CostEstimate(
            flops=2 * rows_here * pairs * degrees * lats_here * ring, bytes_accessed=6 << 20, transcendentals=0),
    )(spec, legendre, wave_of_row, field_slot[None])


def local(spectral, legendre, wave_of_row, row_points, lat_slot, field_slot):
    rows_here, degree_count, _ = legendre.shape
    peers, ring = lax.axis_size("wave"), lax.axis_size("fld")
    spec = jnp.transpose(spectral[0], (0, 2, 1, 3))
    four = spectral_part(spec, jnp.transpose(legendre, (0, 2, 1)), wave_of_row, field_slot, peers, ring)
    waves = wave_of_row.reshape(peers, rows_here).T.reshape(-1)
    grid = zonal(four, waves, row_points, lat_slot, LON)
    return jnp.transpose(grid, (0, 2, 1))[None]


def solution(mesh):
    in_specs = (P("fld", None, None, "wave", None), P("wave", None, "fld"), P(), P(), P(), P())
    out_specs = P("fld", "wave", None, None)
    return jax.shard_map(local, mesh=mesh, in_specs=in_specs, out_specs=out_specs, check_vma=False)
```

```python
import functools
import math

import jax
import jax.numpy as jnp
from jax import lax
from jax.experimental import pallas as pl
from jax.experimental.pallas import tpu as pltpu
from jax.sharding import PartitionSpec as P

LANES = 128
SUBLANES = 8
TOGETHER = 2
MESSAGE = 16
BUNDLES = tuple((c, 1) for c in range(5))
COARSE = 48


def turn(product, points, inverse):
    residue = product - jnp.round(product * inverse) * points
    x = residue * inverse * (math.pi / 2)
    y = x * x
    s = x * (1.0 + y * (-1.0 / 6 + y * (1.0 / 120 + y * (-1.0 / 5040))))
    c = 1.0 + y * (-0.5 + y * (1.0 / 24 + y * (-1.0 / 720 + y * (1.0 / 40320))))
    for _ in range(2):
        c, s = 1.0 - 2.0 * s * s, 2.0 * s * c
    return c, s


def times(a, b):
    return a[0] * b[0] - a[1] * b[1], a[0] * b[1] + a[1] * b[0]


def powers(base, count):
    one = (jnp.ones_like(base[0]), jnp.zeros_like(base[0]))
    out = [one, base]
    for i in range(2, count):
        out.append(times(out[i // 2], out[i - i // 2]))
    return out[:count]


def dot_nt(a, b):
    return lax.dot_general(a, b, (((1,), (1,)), ((), ())), preferred_element_type=jnp.float32)


def zonal_kernel(
    four_ref, wave_ref, points_ref, slot_ref, out_ref,
    live, npts, place, wide, held, inner_c, inner_s, step_c, step_s, outer_c, outer_s, leap_c, leap_s, lead_r, lead_i, left_a, left_b, table_a, table_b, rows,
):
    lat = slot_ref.shape[1]
    waves = wave_ref.shape[1]
    tiles = waves // LANES
    lon = out_ref.shape[1]
    blocks = pl.cdiv(lon, LANES)
    bf16, f32 = jnp.bfloat16, jnp.float32
    left, table = (left_a, left_b), (table_a, table_b)

    row_i = lax.broadcasted_iota(jnp.int32, (lat, lat), 0)
    eye = jnp.where(row_i == lax.broadcasted_iota(jnp.int32, (lat, lat), 1), 1.0, 0.0)
    count = points_ref[...].astype(f32)
    count_down = jnp.sum(eye * count, axis=1, keepdims=True)
    rank = jnp.sum(jnp.where(count_down < count, 1.0, 0.0), axis=0, keepdims=True)
    order = jnp.where(row_i.astype(f32) == rank, 1.0, 0.0)
    npts[...] = jnp.broadcast_to(jnp.sum(order * count, axis=1, keepdims=True), (lat, LANES))
    order = order.astype(bf16)
    in_slot = jnp.where(row_i == slot_ref[...], 1.0, 0.0).astype(bf16)
    place[...] = jnp.dot(order, in_slot, preferred_element_type=f32).astype(bf16)
    sources = four_ref.shape[0]
    for chunk in range(four_ref.shape[1] // MESSAGE):
        wide[...] = four_ref[:, pl.ds(chunk * MESSAGE, MESSAGE), :].astype(f32).reshape(wide.shape)
        for part in range(4):
            for r in range(2):
                halves = [wide[pl.ds(part * 4 + r * 2 + h, sources, stride=MESSAGE), :] for h in range(2)]
                held[part, pl.ds((chunk * 2 + r) * sources, sources), :] = jnp.concatenate(
                    halves, axis=1).astype(bf16)
    for part in range(4):
        moved = dot_nt(order, held[part])
        for t in range(tiles):
            live[part, t] = moved[:, t * LANES:(t + 1) * LANES]

    groups = SUBLANES // TOGETHER

    def multiply(t0, buf, far_count):
        count = 16 * far_count
        used, half = pl.ds(0, TOGETHER * count), LANES // 2
        even = dot_nt(left[buf][used, :waves], table[buf][:, :waves])
        odd = dot_nt(left[buf][used, waves:], table[buf][:, waves:])
        for l in range(TOGETHER):
            e = even[l * count:(l + 1) * count, l * half:(l + 1) * half]
            o = odd[l * count:(l + 1) * count, l * half:(l + 1) * half]
            rows[pl.ds(t0 + l, count, stride=lat), :] = jnp.concatenate([e - o, e + o], axis=1)

    def block(i, carry, far_count, first):
        middle_step = far_count // 2 - 1
        s0 = pl.multiple_of(i * SUBLANES, SUBLANES)
        points = npts[pl.ds(s0, SUBLANES), :]
        inverse = 1.0 / points
        for t in range(tiles):
            m = jnp.broadcast_to(wave_ref[:, t * LANES:(t + 1) * LANES].astype(f32), points.shape)
            weight = jnp.where(2.0 * m < points, jnp.where(m == 0.0, 1.0, 2.0), 0.0)
            half = turn(m, 2.0 * points, 0.5 * inverse)
            near = powers(times(half, half), 9)
            steps = powers(near[8], 5)
            for j, (c, s) in enumerate(steps):
                step_c[t, pl.ds(j * 8, 8), :] = c
                step_s[t, pl.ds(j * 8, 8), :] = s
            middle = times(half, steps[4])
            for j, w in enumerate(near[:8]):
                c, s = times(middle, w) if j else middle
                inner_c[t, pl.ds(j * 8, 8), :] = c
                inner_s[t, pl.ds(j * 8, 8), :] = s
            centre = times(times(steps[4], steps[4]), (half[0], -half[1]))
            outer = powers(turn(m * 128.0, points, inverse), 9)
            for j, (c, s) in enumerate(outer[:8]):
                outer_c[t, pl.ds(j * 8, 8), :] = c
                outer_s[t, pl.ds(j * 8, 8), :] = s
            far = powers(outer[8], far_count - middle_step)
            for j, (c, s) in enumerate(far[1:]):
                leap_c[t, pl.ds(j * 8, 8), :] = c
                leap_s[t, pl.ds(j * 8, 8), :] = s
            if middle_step:
                centre = times(centre, far[middle_step])
            for p in range(2):
                value = (
                    live[2 * p, t, pl.ds(s0, SUBLANES), :] * weight,
                    live[2 * p + 1, t, pl.ds(s0, SUBLANES), :] * weight,
                )
                r, im = times(value, centre)
                lead_r[t, pl.ds(p * 8, 8), :] = r
                lead_i[t, pl.ds(p * 8, 8), :] = im

        def make(l, buf):
            low, high = l % TOGETHER * (LANES // 2), l % TOGETHER * 16 * far_count

            def bcast(ref, t, row):
                return ref[t, pl.ds(row * 8 + l, 8, stride=0), :]

            def spread(ref, t):
                return ref[t, pl.ds(l, 8, stride=8), :]

            for t in range(tiles):
                ic, isn = spread(inner_c, t), spread(inner_s, t)
                cs, ss = [None] * 8, [None] * 8
                cs[4], ss[4] = ic, isn
                for j in range(1, 5):
                    wc, ws = bcast(step_c, t, j), bcast(step_s, t, j)
                    a, b, c, d = ic * wc, isn * ws, isn * wc, ic * ws
                    if j < 4:
                        cs[4 + j], ss[4 + j] = a - b, c + d
                    cs[4 - j], ss[4 - j] = a + b, c - d
                here = pl.ds(t * LANES, LANES)
                there = pl.ds(waves + t * LANES, LANES)
                for q in range(4):
                    table[buf][pl.ds(low + q * 16, 16), here] = jnp.concatenate(
                        [cs[2 * q], cs[2 * q + 1]], axis=0).astype(bf16)
                    table[buf][pl.ds(low + q * 16, 16), there] = jnp.concatenate(
                        [ss[2 * q], ss[2 * q + 1]], axis=0).astype(bf16)
                oc, os = spread(outer_c, t), spread(outer_s, t)
                parts = [[None] * far_count for _ in range(2)]
                for p in range(2):
                    parts[p][middle_step] = times(
                        (bcast(lead_r, t, p), bcast(lead_i, t, p)), (oc, os))
                for j in range(1, far_count - middle_step):
                    wc, ws = bcast(leap_c, t, j - 1), bcast(leap_s, t, j - 1)
                    for p in range(2):
                        r, im = parts[p][middle_step]
                        a, b, c, d = r * wc, im * ws, im * wc, r * ws
                        parts[p][middle_step + j] = (a - b, c + d)
                        if j <= middle_step:
                            parts[p][middle_step - j] = (a + b, c - d)
                for q in range(far_count):
                    for i, where in enumerate((here, there)):
                        left[buf][pl.ds(high + q * 16, 16), where] = jnp.concatenate(
                            [parts[0][q][i], parts[1][q][i]], axis=0).astype(bf16)

        for g in range(groups):
            for l in range(g * TOGETHER, (g + 1) * TOGETHER):
                make(l, g % 2)
            if g:
                multiply(s0 + (g - 1) * TOGETHER, (g - 1) % 2, far_count)
            else:
                before = jnp.where(i > first, s0 - TOGETHER, s0 + SUBLANES - TOGETHER)
                multiply(before, (groups - 1) % 2, far_count)
        return carry

    start = 0
    for far_count in range(2, COARSE // 8 + 1, 2):
        if far_count == COARSE // 8:
            end = lat // SUBLANES
        else:
            fits = jnp.where(count <= far_count * 1024.0, 1.0, 0.0)
            end = jnp.sum(fits).astype(jnp.int32) // SUBLANES
        lax.fori_loop(start, end, functools.partial(block, far_count=far_count, first=start), 0)

        @pl.when(end > start)
        def _(end=end, far_count=far_count):
            multiply(end * SUBLANES - TOGETHER, (groups - 1) % 2, far_count)

        start = end

    def longitude_of(shape):
        lane = lax.broadcasted_iota(jnp.int32, shape, 1)
        return jnp.where(lane < LANES // 2, lane + LANES // 2, LANES - 1 - lane)

    square = (LANES, LANES)
    small = jnp.where(lax.broadcasted_iota(jnp.int32, square, 0) == longitude_of(square), 1.0, 0.0).astype(bf16)
    lane = longitude_of((lat, LANES)).astype(f32)

    def turned(p, a):
        at = (a // 8) * 16 + p * 8 + a % 8
        value = rows[pl.ds(pl.multiple_of(at * lat, lat), lat), :]
        first = jnp.float32(a * LANES) if isinstance(a, int) else (a * LANES).astype(f32)
        value = jnp.where(lane + first < npts[...], value, 0.0).astype(bf16)
        value = dot_nt(small, value).astype(bf16)
        return jnp.dot(value, place[...], preferred_element_type=f32).astype(bf16)

    for p in range(2):
        def whole(h, carry, p=p):
            for a in (2 * h, 2 * h + 1):
                out_ref[p, pl.ds(pl.multiple_of(a * LANES, LANES), LANES), :] = turned(p, a)
            return carry

        lax.fori_loop(0, (blocks - 1) // 2, whole, 0)
        for a in range((blocks - 1) // 2 * 2, blocks):
            first = a * LANES
            size = min(LANES, lon - first)
            out_ref[p, first:first + size, :] = turned(p, a)[:size]


def zonal(four, wave_of_row, row_points, lat_slot, lon):
    waves, lat = wave_of_row.shape[0], lat_slot.shape[0]
    tiles = waves // LANES
    f32 = jnp.float32
    vmem = pl.BlockSpec(memory_space=pltpu.VMEM)

    left_shape = pltpu.VMEM((TOGETHER * 2 * COARSE, 2 * waves), jnp.bfloat16)
    table_shape = pltpu.VMEM((TOGETHER * LANES // 2, 2 * waves), jnp.bfloat16)

    def scratch(count):
        return pltpu.VMEM((tiles, count * 8, LANES), f32)

    return pl.pallas_call(
        zonal_kernel,
        out_shape=jax.ShapeDtypeStruct((2, lon, lat), jnp.bfloat16),
        in_specs=[vmem] * 4,
        out_specs=vmem,
        scratch_shapes=[
            pltpu.VMEM((4, tiles, lat, LANES), f32),
            pltpu.VMEM((lat, LANES), f32),
            pltpu.VMEM((lat, lat), jnp.bfloat16),
            pltpu.VMEM((four.shape[0] * MESSAGE, LANES), f32),
            pltpu.VMEM((4, waves, lat), jnp.bfloat16),
            scratch(8), scratch(8), scratch(5), scratch(5), scratch(8), scratch(8),
            scratch(COARSE // 16), scratch(COARSE // 16), scratch(2), scratch(2),
            left_shape, left_shape, table_shape, table_shape,
            pltpu.VMEM((2 * COARSE * lat, LANES), f32),
        ],
        compiler_params=pltpu.CompilerParams(vmem_limit_bytes=48 * 1024 * 1024),
        cost_estimate=pl.CostEstimate(
            flops=2 * lat * 2 * COARSE * LANES * 2 * waves, bytes_accessed=7 << 20, transcendentals=0
        ),
    )(four, wave_of_row[None], row_points[None], lat_slot[None])


LON = 5136
MESH = pl.DeviceIdType.MESH


def spectral_kernel(
    spec_hbm, leg_ref, wave_ref, field_ref, recv_ref,
    spec_ref, legs, swap, lefts, mixed, outbox,
    spec_sem, own_sem, send_a, recv_a, send_f, recv_f, send_m, recv_m, keep_m,
):
    bf16, f32 = jnp.bfloat16, jnp.float32
    me, y = lax.axis_index("wave"), lax.axis_index("fld")
    peers, ring = lax.axis_size("wave"), lax.axis_size("fld")
    right, left = lax.rem(y + 1, ring), lax.rem(y + ring - 1, ring)
    rows_here, lats_here, degrees = leg_ref.shape
    chunks = rows_here // 2
    pairs = spec_ref.shape[0] * spec_ref.shape[2]

    def there(k):
        other = me + k
        return jnp.where(other >= peers, other - peers, other)

    barrier = pltpu.get_barrier_semaphore()

    def greet(k, carry):
        pl.semaphore_signal(barrier, inc=1, device_id=(there(k), y), device_id_type=MESH)
        return carry

    for side in (right, left):
        pl.semaphore_signal(barrier, inc=1, device_id=(me, side), device_id_type=MESH)
    lax.fori_loop(1, peers, greet, 0, unroll=9)

    def own():
        return pltpu.make_async_copy(leg_ref, legs.at[y], own_sem)

    def first(c, side):
        at = pl.ds(2 * c, 2)
        return pltpu.make_async_remote_copy(
            src_ref=leg_ref.at[at], dst_ref=legs.at[y, at],
            send_sem=send_a.at[side, c], recv_sem=recv_a.at[side, c],
            device_id=(me, (right, left)[side]), device_id_type=MESH)

    def second(c, side):
        block, at = (left, right)[side], pl.ds(2 * c + side, 1)
        return pltpu.make_async_remote_copy(
            src_ref=legs.at[block, at], dst_ref=legs.at[block, at],
            send_sem=send_f.at[side, c], recv_sem=recv_f.at[side, c],
            device_id=(me, (right, left)[side]), device_id_type=MESH)

    def rows_of(g):
        return pl.ds(BUNDLES[g][0] * MESSAGE, BUNDLES[g][1] * MESSAGE)

    def message(g, k):
        other = there(k)
        return pltpu.make_async_remote_copy(
            src_ref=outbox.at[other, rows_of(g)], dst_ref=recv_ref.at[me, rows_of(g)],
            send_sem=send_m.at[g], recv_sem=recv_m.at[g],
            device_id=(other, y), device_id_type=MESH)

    def all_messages(g):
        some = pl.ds(0, peers - 1)
        return pltpu.make_async_remote_copy(
            src_ref=outbox.at[some, rows_of(g)], dst_ref=recv_ref.at[some, rows_of(g)],
            send_sem=send_m.at[g], recv_sem=recv_m.at[g],
            device_id=(there(1), y), device_id_type=MESH)

    def kept(g):
        return pltpu.make_async_copy(outbox.at[me, rows_of(g)], recv_ref.at[me, rows_of(g)], keep_m.at[g])

    def spec_copy():
        return pltpu.make_async_copy(spec_hbm, spec_ref, spec_sem)

    spec_copy().start()
    own().start()

    row_i = lax.broadcasted_iota(jnp.int32, (pairs, pairs), 0)
    col_i = lax.broadcasted_iota(jnp.int32, (pairs, pairs), 1)
    eye = jnp.where(row_i == col_i, 1.0, 0.0).astype(bf16)
    twice_i = lax.broadcasted_iota(jnp.int32, (pairs // 2, pairs), 1)
    twice = jnp.where(
        lax.broadcasted_iota(jnp.int32, (pairs // 2, pairs), 0) == twice_i // 2, 1.0, 0.0).astype(bf16)
    fields = jnp.broadcast_to(field_ref[...].astype(f32), (8, pairs // 2)).astype(bf16)
    wanted = 2.0 * jnp.dot(fields, twice, preferred_element_type=f32)[0:1]
    wanted = wanted + (col_i[0:1] % 2).astype(f32)
    swap[...] = dot_nt(eye, jnp.where(row_i.astype(f32) == wanted, 1.0, 0.0).astype(bf16)).astype(bf16)

    own().wait()
    pl.semaphore_wait(barrier, peers + 1)
    for side in range(2):
        first(0, side).start()
    spec_copy().wait()

    def pass_on(c):
        for side in range(2):
            first(c, side).wait_recv()
        for side in range(2):
            second(c, side).start()

        @pl.when(c < chunks - 1)
        def _():
            for side in range(2):
                first(c + 1, side).start()

    pass_on(0)

    def step(c, carry):
        @pl.when(c < chunks - 1)
        def _():
            pass_on(c + 1)

        for r in range(2):
            lefts[r] = spec_ref[:, 2 * c + r].reshape(pairs, degrees)
        for side in range(2):
            second(c, side).wait_recv()
        degree = lax.broadcasted_iota(jnp.int32, (ring * lats_here, degrees), 1)
        for r in range(2):
            row = 2 * c + r
            values = jnp.concatenate([legs[g, row] for g in range(ring)], axis=0)
            values = jnp.where(degree >= wave_ref[me * rows_here + row], values.astype(f32), 0.0).astype(bf16)
            fourier = dot_nt(lefts[r], values).astype(bf16)
            fourier = jnp.dot(swap[...], fourier, preferred_element_type=f32)
            for h in range(2):
                mixed[pl.ds(r * 2 + h, pairs, stride=4), :] = fourier[:, h * LANES:(h + 1) * LANES]
        outbox[:, pl.ds(pl.multiple_of(c * MESSAGE, MESSAGE), MESSAGE), :] = mixed[...].astype(bf16).reshape(
            peers, MESSAGE, LANES)
        return carry

    for g, (c0, size) in enumerate(BUNDLES):
        lax.fori_loop(c0, c0 + size, step, 0)
        kept(g).start()

        def post(k, carry, g=g):
            message(g, k).start()
            return carry

        lax.fori_loop(1, peers, post, 0, unroll=9)

    def finish(c, carry):
        for side in range(2):
            first(c, side).wait_send()
            second(c, side).wait_send()
        return carry

    lax.fori_loop(0, chunks, finish, 0)
    for g in range(len(BUNDLES)):
        kept(g).wait()
        all_messages(g).wait()


def spectral_part(spec, legendre, wave_of_row, field_slot, peers, ring):
    pairs, degrees = spec.shape[0] * spec.shape[2], spec.shape[3]
    rows_here = spec.shape[1]
    lats_here = legendre.shape[1]
    chunks = rows_here // 2
    bf16 = jnp.bfloat16
    vmem = pl.BlockSpec(memory_space=pltpu.VMEM)
    hbm = pl.BlockSpec(memory_space=pltpu.HBM)
    pairs_sem = pltpu.SemaphoreType.DMA((2, chunks))
    bundle_sem = pltpu.SemaphoreType.DMA((len(BUNDLES),))
    return pl.pallas_call(
        spectral_kernel,
        out_shape=jax.ShapeDtypeStruct((peers, chunks * MESSAGE, LANES), bf16),
        in_specs=[hbm, hbm, pl.BlockSpec(memory_space=pltpu.SMEM), vmem],
        out_specs=pl.BlockSpec(memory_space=pl.ANY),
        scratch_shapes=[
            pltpu.VMEM(spec.shape, bf16),
            pltpu.VMEM((ring, rows_here, lats_here, degrees), bf16),
            pltpu.VMEM((pairs, pairs), bf16),
            pltpu.VMEM((2, pairs, degrees), bf16),
            pltpu.VMEM((peers * MESSAGE, LANES), jnp.float32),
            pltpu.VMEM((peers, chunks * MESSAGE, LANES), bf16),
            pltpu.SemaphoreType.DMA,
            pltpu.SemaphoreType.DMA,
            pairs_sem, pairs_sem, pairs_sem, pairs_sem, bundle_sem, bundle_sem, bundle_sem,
        ],
        compiler_params=pltpu.CompilerParams(
            collective_id=0, has_side_effects=True, vmem_limit_bytes=60 * 1024 * 1024),
        cost_estimate=pl.CostEstimate(
            flops=2 * rows_here * pairs * degrees * lats_here * ring, bytes_accessed=6 << 20, transcendentals=0),
    )(spec, legendre, wave_of_row, field_slot[None])


def local(spectral, legendre, wave_of_row, row_points, lat_slot, field_slot):
    rows_here, degree_count, _ = legendre.shape
    peers, ring = lax.axis_size("wave"), lax.axis_size("fld")
    spec = jnp.transpose(spectral[0], (0, 2, 1, 3))
    four = spectral_part(spec, jnp.transpose(legendre, (0, 2, 1)), wave_of_row, field_slot, peers, ring)
    waves = wave_of_row.reshape(peers, rows_here).T.reshape(-1)
    grid = zonal(four, waves, row_points, lat_slot, LON)
    return jnp.transpose(grid, (0, 2, 1))[None]


def solution(mesh):
    in_specs = (P("fld", None, None, "wave", None), P("wave", None, "fld"), P(), P(), P(), P())
    out_specs = P("fld", "wave", None, None)
    return jax.shard_map(local, mesh=mesh, in_specs=in_specs, out_specs=out_specs, check_vma=False)
```

```python
import functools
import math

import jax
import jax.numpy as jnp
from jax import lax
from jax.experimental import pallas as pl
from jax.experimental.pallas import tpu as pltpu
from jax.sharding import PartitionSpec as P

LANES = 128
SUBLANES = 8
STEP = 5
PAD = 8
TOGETHER = 2
MESSAGE = 16
BUNDLES = tuple((c, 1) for c in range(5))
COARSE = 48


def turn(product, points, inverse):
    residue = product - jnp.round(product * inverse) * points
    x = residue * inverse * (math.pi / 2)
    y = x * x
    s = x * (1.0 + y * (-1.0 / 6 + y * (1.0 / 120 + y * (-1.0 / 5040))))
    c = 1.0 + y * (-0.5 + y * (1.0 / 24 + y * (-1.0 / 720 + y * (1.0 / 40320))))
    for _ in range(2):
        c, s = 1.0 - 2.0 * s * s, 2.0 * s * c
    return c, s


def times(a, b):
    return a[0] * b[0] - a[1] * b[1], a[0] * b[1] + a[1] * b[0]


def powers(base, count):
    one = (jnp.ones_like(base[0]), jnp.zeros_like(base[0]))
    out = [one, base]
    for i in range(2, count):
        out.append(times(out[i // 2], out[i - i // 2]))
    return out[:count]


def dot_nt(a, b):
    return lax.dot_general(a, b, (((1,), (1,)), ((), ())), preferred_element_type=jnp.float32)


def zonal_kernel(
    four_ref, wave_ref, points_ref, slot_ref, out_ref,
    live, npts, place, wide, held, inner_c, inner_s, step_c, step_s, outer_c, outer_s, leap_c, leap_s, lead_r, lead_i, left_a, left_b, table_a, table_b, rows,
):
    lat = slot_ref.shape[1]
    waves = wave_ref.shape[1]
    tiles = waves // LANES
    lon = out_ref.shape[1]
    blocks = pl.cdiv(lon, LANES)
    bf16, f32 = jnp.bfloat16, jnp.float32
    left, table = (left_a, left_b), (table_a, table_b)

    row_i = lax.broadcasted_iota(jnp.int32, (lat, lat), 0)
    eye = jnp.where(row_i == lax.broadcasted_iota(jnp.int32, (lat, lat), 1), 1.0, 0.0)
    count = points_ref[...].astype(f32)
    count_down = jnp.sum(eye * count, axis=1, keepdims=True)
    rank = jnp.sum(jnp.where(count_down < count, 1.0, 0.0), axis=0, keepdims=True)
    order = jnp.where(row_i.astype(f32) == rank, 1.0, 0.0)
    npts[...] = jnp.broadcast_to(jnp.sum(order * count, axis=1, keepdims=True), (lat, LANES))
    order = order.astype(bf16)
    in_slot = jnp.where(row_i == slot_ref[...], 1.0, 0.0).astype(bf16)
    place[...] = jnp.dot(order, in_slot, preferred_element_type=f32).astype(bf16)
    sources = four_ref.shape[0]
    for chunk in range(four_ref.shape[1] // MESSAGE):
        wide[...] = four_ref[:, pl.ds(chunk * MESSAGE, MESSAGE), :].astype(f32).reshape(wide.shape)
        for part in range(4):
            for r in range(2):
                halves = [wide[pl.ds(part * 4 + r * 2 + h, sources, stride=MESSAGE), :] for h in range(2)]
                held[part, pl.ds((chunk * 2 + r) * sources, sources), :] = jnp.concatenate(
                    halves, axis=1).astype(bf16)
    for part in range(4):
        moved = dot_nt(order, held[part])
        for t in range(tiles):
            live[part, t] = moved[:, t * LANES:(t + 1) * LANES]

    groups = SUBLANES // TOGETHER

    def multiply(t0, buf, far_count):
        count = 16 * far_count
        used, half = pl.ds(0, TOGETHER * count), LANES // 2
        even = dot_nt(left[buf][used, :waves], table[buf][:, :waves])
        odd = dot_nt(left[buf][used, waves:], table[buf][:, waves:])
        for l in range(TOGETHER):
            e = even[l * count:(l + 1) * count, l * half:(l + 1) * half]
            o = odd[l * count:(l + 1) * count, l * half:(l + 1) * half]
            rows[pl.ds(t0 + l, count, stride=lat + PAD), :] = jnp.concatenate([e - o, e + o], axis=1)

    def block(i, carry, far_count, first):
        middle_step = far_count // 2 - 1
        s0 = pl.multiple_of(i * SUBLANES, SUBLANES)
        points = npts[pl.ds(s0, SUBLANES), :]
        inverse = 1.0 / points
        for t in range(tiles):
            m = jnp.broadcast_to(wave_ref[:, t * LANES:(t + 1) * LANES].astype(f32), points.shape)
            weight = jnp.where(2.0 * m < points, jnp.where(m == 0.0, 1.0, 2.0), 0.0)
            half = turn(m, 2.0 * points, 0.5 * inverse)
            near = powers(times(half, half), 9)
            steps = powers(near[8], 5)
            for j, (c, s) in enumerate(steps):
                step_c[t, pl.ds(j * 8, 8), :] = c
                step_s[t, pl.ds(j * 8, 8), :] = s
            middle = times(half, steps[4])
            for j, w in enumerate(near[:8]):
                c, s = times(middle, w) if j else middle
                inner_c[t, pl.ds(j * 8, 8), :] = c
                inner_s[t, pl.ds(j * 8, 8), :] = s
            centre = times(times(steps[4], steps[4]), (half[0], -half[1]))
            outer = powers(turn(m * 128.0, points, inverse), 9)
            for j, (c, s) in enumerate(outer[:8]):
                outer_c[t, pl.ds(j * 8, 8), :] = c
                outer_s[t, pl.ds(j * 8, 8), :] = s
            far = powers(outer[8], far_count - middle_step)
            for j, (c, s) in enumerate(far[1:]):
                leap_c[t, pl.ds(j * 8, 8), :] = c
                leap_s[t, pl.ds(j * 8, 8), :] = s
            if middle_step:
                centre = times(centre, far[middle_step])
            for p in range(2):
                value = (
                    live[2 * p, t, pl.ds(s0, SUBLANES), :] * weight,
                    live[2 * p + 1, t, pl.ds(s0, SUBLANES), :] * weight,
                )
                r, im = times(value, centre)
                lead_r[t, pl.ds(p * 8, 8), :] = r
                lead_i[t, pl.ds(p * 8, 8), :] = im

        def make(l, buf):
            low, high = l % TOGETHER * (LANES // 2), l % TOGETHER * 16 * far_count

            def bcast(ref, t, row):
                return ref[t, pl.ds(row * 8 + l, 8, stride=0), :]

            def spread(ref, t):
                return ref[t, pl.ds(l, 8, stride=8), :]

            for t in range(tiles):
                ic, isn = spread(inner_c, t), spread(inner_s, t)
                cs, ss = [None] * 8, [None] * 8
                cs[4], ss[4] = ic, isn
                for j in range(1, 5):
                    wc, ws = bcast(step_c, t, j), bcast(step_s, t, j)
                    a, b, c, d = ic * wc, isn * ws, isn * wc, ic * ws
                    if j < 4:
                        cs[4 + j], ss[4 + j] = a - b, c + d
                    cs[4 - j], ss[4 - j] = a + b, c - d
                here = pl.ds(t * LANES, LANES)
                there = pl.ds(waves + t * LANES, LANES)
                for q in range(4):
                    table[buf][pl.ds(low + q * 16, 16), here] = jnp.concatenate(
                        [cs[2 * q], cs[2 * q + 1]], axis=0).astype(bf16)
                    table[buf][pl.ds(low + q * 16, 16), there] = jnp.concatenate(
                        [ss[2 * q], ss[2 * q + 1]], axis=0).astype(bf16)
                oc, os = spread(outer_c, t), spread(outer_s, t)
                parts = [[None] * far_count for _ in range(2)]
                for p in range(2):
                    parts[p][middle_step] = times(
                        (bcast(lead_r, t, p), bcast(lead_i, t, p)), (oc, os))
                for j in range(1, far_count - middle_step):
                    wc, ws = bcast(leap_c, t, j - 1), bcast(leap_s, t, j - 1)
                    for p in range(2):
                        r, im = parts[p][middle_step]
                        a, b, c, d = r * wc, im * ws, im * wc, r * ws
                        parts[p][middle_step + j] = (a - b, c + d)
                        if j <= middle_step:
                            parts[p][middle_step - j] = (a + b, c - d)
                for q in range(far_count):
                    for i, where in enumerate((here, there)):
                        left[buf][pl.ds(high + q * 16, 16), where] = jnp.concatenate(
                            [parts[0][q][i], parts[1][q][i]], axis=0).astype(bf16)

        for g in range(groups):
            for l in range(g * TOGETHER, (g + 1) * TOGETHER):
                make(l, g % 2)
            if g:
                multiply(s0 + (g - 1) * TOGETHER, (g - 1) % 2, far_count)
            else:
                before = jnp.where(i > first, s0 - TOGETHER, s0 + SUBLANES - TOGETHER)
                multiply(before, (groups - 1) % 2, far_count)
        return carry

    start = 0
    for far_count in range(2, COARSE // 8 + 1, 2):
        if far_count == COARSE // 8:
            end = lat // SUBLANES
        else:
            fits = jnp.where(count <= far_count * 1024.0, 1.0, 0.0)
            end = jnp.sum(fits).astype(jnp.int32) // SUBLANES
        lax.fori_loop(start, end, functools.partial(block, far_count=far_count, first=start), 0)

        @pl.when(end > start)
        def _(end=end, far_count=far_count):
            multiply(end * SUBLANES - TOGETHER, (groups - 1) % 2, far_count)

        start = end

    def longitude_of(shape):
        lane = lax.broadcasted_iota(jnp.int32, shape, 1)
        return jnp.where(lane < LANES // 2, lane + LANES // 2, LANES - 1 - lane)

    square = (LANES, LANES)
    small = jnp.where(lax.broadcasted_iota(jnp.int32, square, 0) == longitude_of(square), 1.0, 0.0).astype(bf16)
    npts[...] = npts[...] - longitude_of((lat, LANES)).astype(f32)

    def turned(p, a):
        at = (a // 8) * 16 + p * 8 + a % 8
        value = rows[pl.ds(pl.multiple_of(at * (lat + PAD), 8), lat), :]
        first = jnp.float32(a * LANES) if isinstance(a, int) else (a * LANES).astype(f32)
        return dot_nt(small, jnp.where(npts[...] > first, value, 0.0).astype(bf16)).astype(bf16)

    def placed(values):
        return jnp.dot(jnp.concatenate(values, axis=0), place[...], preferred_element_type=f32).astype(bf16)

    whole_blocks = lon // LANES
    for p in range(2):
        def some(h, carry, p=p):
            out_ref[p, pl.ds(pl.multiple_of(h * STEP * LANES, LANES), STEP * LANES), :] = placed(
                [turned(p, h * STEP + i) for i in range(STEP)])
            return carry

        lax.fori_loop(0, whole_blocks // STEP, some, 0)
        for a in range(whole_blocks // STEP * STEP, blocks):
            size = min(LANES, lon - a * LANES)
            out_ref[p, a * LANES:a * LANES + size, :] = placed([turned(p, a)])[:size]


def zonal(four, wave_of_row, row_points, lat_slot, lon):
    waves, lat = wave_of_row.shape[0], lat_slot.shape[0]
    tiles = waves // LANES
    f32 = jnp.float32
    vmem = pl.BlockSpec(memory_space=pltpu.VMEM)

    left_shape = pltpu.VMEM((TOGETHER * 2 * COARSE, 2 * waves), jnp.bfloat16)
    table_shape = pltpu.VMEM((TOGETHER * LANES // 2, 2 * waves), jnp.bfloat16)

    def scratch(count):
        return pltpu.VMEM((tiles, count * 8, LANES), f32)

    return pl.pallas_call(
        zonal_kernel,
        out_shape=jax.ShapeDtypeStruct((2, lon, lat), jnp.bfloat16),
        in_specs=[vmem] * 4,
        out_specs=vmem,
        scratch_shapes=[
            pltpu.VMEM((4, tiles, lat, LANES), f32),
            pltpu.VMEM((lat, LANES), f32),
            pltpu.VMEM((lat, lat), jnp.bfloat16),
            pltpu.VMEM((four.shape[0] * MESSAGE, LANES), f32),
            pltpu.VMEM((4, waves, lat), jnp.bfloat16),
            scratch(8), scratch(8), scratch(5), scratch(5), scratch(8), scratch(8),
            scratch(COARSE // 16), scratch(COARSE // 16), scratch(2), scratch(2),
            left_shape, left_shape, table_shape, table_shape,
            pltpu.VMEM((2 * COARSE * (lat + PAD), LANES), f32),
        ],
        compiler_params=pltpu.CompilerParams(vmem_limit_bytes=48 * 1024 * 1024),
        cost_estimate=pl.CostEstimate(
            flops=2 * lat * 2 * COARSE * LANES * 2 * waves, bytes_accessed=7 << 20, transcendentals=0
        ),
    )(four, wave_of_row[None], row_points[None], lat_slot[None])


LON = 5136
MESH = pl.DeviceIdType.MESH


def spectral_kernel(
    spec_hbm, leg_ref, wave_ref, field_ref, recv_ref,
    spec_ref, legs, swap, lefts, mixed, outbox,
    spec_sem, own_sem, send_a, recv_a, send_f, recv_f, send_m, recv_m, keep_m,
):
    bf16, f32 = jnp.bfloat16, jnp.float32
    me, y = lax.axis_index("wave"), lax.axis_index("fld")
    peers, ring = lax.axis_size("wave"), lax.axis_size("fld")
    right, left = lax.rem(y + 1, ring), lax.rem(y + ring - 1, ring)
    rows_here, lats_here, degrees = leg_ref.shape
    chunks = rows_here // 2
    pairs = spec_ref.shape[0] * spec_ref.shape[2]

    def there(k):
        other = me + k
        return jnp.where(other >= peers, other - peers, other)

    barrier = pltpu.get_barrier_semaphore()

    def greet(k, carry):
        pl.semaphore_signal(barrier, inc=1, device_id=(there(k), y), device_id_type=MESH)
        return carry

    for side in (right, left):
        pl.semaphore_signal(barrier, inc=1, device_id=(me, side), device_id_type=MESH)
    lax.fori_loop(1, peers, greet, 0, unroll=9)

    def own():
        return pltpu.make_async_copy(leg_ref, legs.at[y], own_sem)

    def first(c, side):
        at = pl.ds(2 * c, 2)
        return pltpu.make_async_remote_copy(
            src_ref=leg_ref.at[at], dst_ref=legs.at[y, at],
            send_sem=send_a.at[side, c], recv_sem=recv_a.at[side, c],
            device_id=(me, (right, left)[side]), device_id_type=MESH)

    def second(c, side):
        block, at = (left, right)[side], pl.ds(2 * c + side, 1)
        return pltpu.make_async_remote_copy(
            src_ref=legs.at[block, at], dst_ref=legs.at[block, at],
            send_sem=send_f.at[side, c], recv_sem=recv_f.at[side, c],
            device_id=(me, (right, left)[side]), device_id_type=MESH)

    def rows_of(g):
        return pl.ds(BUNDLES[g][0] * MESSAGE, BUNDLES[g][1] * MESSAGE)

    def message(g, k):
        other = there(k)
        return pltpu.make_async_remote_copy(
            src_ref=outbox.at[other, rows_of(g)], dst_ref=recv_ref.at[me, rows_of(g)],
            send_sem=send_m.at[g], recv_sem=recv_m.at[g],
            device_id=(other, y), device_id_type=MESH)

    def all_messages(g):
        some = pl.ds(0, peers - 1)
        return pltpu.make_async_remote_copy(
            src_ref=outbox.at[some, rows_of(g)], dst_ref=recv_ref.at[some, rows_of(g)],
            send_sem=send_m.at[g], recv_sem=recv_m.at[g],
            device_id=(there(1), y), device_id_type=MESH)

    def kept(g):
        return pltpu.make_async_copy(outbox.at[me, rows_of(g)], recv_ref.at[me, rows_of(g)], keep_m.at[g])

    def spec_copy():
        return pltpu.make_async_copy(spec_hbm, spec_ref, spec_sem)

    spec_copy().start()
    own().start()

    row_i = lax.broadcasted_iota(jnp.int32, (pairs, pairs), 0)
    col_i = lax.broadcasted_iota(jnp.int32, (pairs, pairs), 1)
    eye = jnp.where(row_i == col_i, 1.0, 0.0).astype(bf16)
    twice_i = lax.broadcasted_iota(jnp.int32, (pairs // 2, pairs), 1)
    twice = jnp.where(
        lax.broadcasted_iota(jnp.int32, (pairs // 2, pairs), 0) == twice_i // 2, 1.0, 0.0).astype(bf16)
    fields = jnp.broadcast_to(field_ref[...].astype(f32), (8, pairs // 2)).astype(bf16)
    wanted = 2.0 * jnp.dot(fields, twice, preferred_element_type=f32)[0:1]
    wanted = wanted + (col_i[0:1] % 2).astype(f32)
    swap[...] = dot_nt(eye, jnp.where(row_i.astype(f32) == wanted, 1.0, 0.0).astype(bf16)).astype(bf16)

    own().wait()
    pl.semaphore_wait(barrier, peers + 1)
    for side in range(2):
        first(0, side).start()
    spec_copy().wait()

    def pass_on(c):
        for side in range(2):
            first(c, side).wait_recv()
        for side in range(2):
            second(c, side).start()

        @pl.when(c < chunks - 1)
        def _():
            for side in range(2):
                first(c + 1, side).start()

    pass_on(0)

    def step(c, carry):
        @pl.when(c < chunks - 1)
        def _():
            pass_on(c + 1)

        for r in range(2):
            lefts[r] = spec_ref[:, 2 * c + r].reshape(pairs, degrees)
        for side in range(2):
            second(c, side).wait_recv()
        degree = lax.broadcasted_iota(jnp.int32, (ring * lats_here, degrees), 1)
        for r in range(2):
            row = 2 * c + r
            values = jnp.concatenate([legs[g, row] for g in range(ring)], axis=0)
            values = jnp.where(degree >= wave_ref[me * rows_here + row], values.astype(f32), 0.0).astype(bf16)
            fourier = dot_nt(lefts[r], values).astype(bf16)
            fourier = jnp.dot(swap[...], fourier, preferred_element_type=f32)
            for h in range(2):
                mixed[pl.ds(r * 2 + h, pairs, stride=4), :] = fourier[:, h * LANES:(h + 1) * LANES]
        outbox[:, pl.ds(pl.multiple_of(c * MESSAGE, MESSAGE), MESSAGE), :] = mixed[...].astype(bf16).reshape(
            peers, MESSAGE, LANES)
        return carry

    for g, (c0, size) in enumerate(BUNDLES):
        lax.fori_loop(c0, c0 + size, step, 0)
        kept(g).start()

        message(g, peers // 2).start()

        def post(k, carry, g=g):
            message(g, peers // 2 - k).start()
            message(g, peers // 2 + k).start()
            return carry

        lax.fori_loop(1, peers // 2, post, 0, unroll=4)

    def finish(c, carry):
        for side in range(2):
            first(c, side).wait_send()
            second(c, side).wait_send()
        return carry

    lax.fori_loop(0, chunks, finish, 0)
    for g in range(len(BUNDLES)):
        kept(g).wait()
        all_messages(g).wait()


def spectral_part(spec, legendre, wave_of_row, field_slot, peers, ring):
    pairs, degrees = spec.shape[0] * spec.shape[2], spec.shape[3]
    rows_here = spec.shape[1]
    lats_here = legendre.shape[1]
    chunks = rows_here // 2
    bf16 = jnp.bfloat16
    vmem = pl.BlockSpec(memory_space=pltpu.VMEM)
    hbm = pl.BlockSpec(memory_space=pltpu.HBM)
    pairs_sem = pltpu.SemaphoreType.DMA((2, chunks))
    bundle_sem = pltpu.SemaphoreType.DMA((len(BUNDLES),))
    return pl.pallas_call(
        spectral_kernel,
        out_shape=jax.ShapeDtypeStruct((peers, chunks * MESSAGE, LANES), bf16),
        in_specs=[hbm, hbm, pl.BlockSpec(memory_space=pltpu.SMEM), vmem],
        out_specs=pl.BlockSpec(memory_space=pl.ANY),
        scratch_shapes=[
            pltpu.VMEM(spec.shape, bf16),
            pltpu.VMEM((ring, rows_here, lats_here, degrees), bf16),
            pltpu.VMEM((pairs, pairs), bf16),
            pltpu.VMEM((2, pairs, degrees), bf16),
            pltpu.VMEM((peers * MESSAGE, LANES), jnp.float32),
            pltpu.VMEM((peers, chunks * MESSAGE, LANES), bf16),
            pltpu.SemaphoreType.DMA,
            pltpu.SemaphoreType.DMA,
            pairs_sem, pairs_sem, pairs_sem, pairs_sem, bundle_sem, bundle_sem, bundle_sem,
        ],
        compiler_params=pltpu.CompilerParams(
            collective_id=0, has_side_effects=True, vmem_limit_bytes=60 * 1024 * 1024),
        cost_estimate=pl.CostEstimate(
            flops=2 * rows_here * pairs * degrees * lats_here * ring, bytes_accessed=6 << 20, transcendentals=0),
    )(spec, legendre, wave_of_row, field_slot[None])


def local(spectral, legendre, wave_of_row, row_points, lat_slot, field_slot):
    rows_here, degree_count, _ = legendre.shape
    peers, ring = lax.axis_size("wave"), lax.axis_size("fld")
    spec = jnp.transpose(spectral[0], (0, 2, 1, 3))
    four = spectral_part(spec, jnp.transpose(legendre, (0, 2, 1)), wave_of_row, field_slot, peers, ring)
    waves = wave_of_row.reshape(peers, rows_here).T.reshape(-1)
    grid = zonal(four, waves, row_points, lat_slot, LON)
    return jnp.transpose(grid, (0, 2, 1))[None]


def solution(mesh):
    in_specs = (P("fld", None, None, "wave", None), P("wave", None, "fld"), P(), P(), P(), P())
    out_specs = P("fld", "wave", None, None)
    return jax.shard_map(local, mesh=mesh, in_specs=in_specs, out_specs=out_specs, check_vma=False)
```

```python
import functools
import math

import jax
import jax.numpy as jnp
from jax import lax
from jax.experimental import pallas as pl
from jax.experimental.pallas import tpu as pltpu
from jax.sharding import PartitionSpec as P

LANES = 128
SUBLANES = 8
STEP = 5
PAD = 8
TOGETHER = 2
MESSAGE = 16
EARLY = 6
BUNDLES = tuple((c, 1) for c in range(5))
COARSE = 48


def turn(product, points, inverse):
    residue = product - jnp.round(product * inverse) * points
    x = residue * inverse * (math.pi / 2)
    y = x * x
    s = x * (1.0 + y * (-1.0 / 6 + y * (1.0 / 120 + y * (-1.0 / 5040))))
    c = 1.0 + y * (-0.5 + y * (1.0 / 24 + y * (-1.0 / 720 + y * (1.0 / 40320))))
    for _ in range(2):
        c, s = 1.0 - 2.0 * s * s, 2.0 * s * c
    return c, s


def times(a, b):
    return a[0] * b[0] - a[1] * b[1], a[0] * b[1] + a[1] * b[0]


def powers(base, count):
    one = (jnp.ones_like(base[0]), jnp.zeros_like(base[0]))
    out = [one, base]
    for i in range(2, count):
        out.append(times(out[i // 2], out[i - i // 2]))
    return out[:count]


def dot_nt(a, b):
    return lax.dot_general(a, b, (((1,), (1,)), ((), ())), preferred_element_type=jnp.float32)


def zonal_kernel(
    four_ref, wave_ref, points_ref, slot_ref, out_ref,
    live, npts, place, wide, held, inner_c, inner_s, step_c, step_s, outer_c, outer_s, leap_c, leap_s, lead_r, lead_i, left_a, left_b, table_a, table_b, rows,
):
    lat = slot_ref.shape[1]
    waves = wave_ref.shape[1]
    tiles = waves // LANES
    lon = out_ref.shape[1]
    blocks = pl.cdiv(lon, LANES)
    bf16, f32 = jnp.bfloat16, jnp.float32
    left, table = (left_a, left_b), (table_a, table_b)

    row_i = lax.broadcasted_iota(jnp.int32, (lat, lat), 0)
    eye = jnp.where(row_i == lax.broadcasted_iota(jnp.int32, (lat, lat), 1), 1.0, 0.0)
    count = points_ref[...].astype(f32)
    count_down = jnp.sum(eye * count, axis=1, keepdims=True)
    rank = jnp.sum(jnp.where(count_down < count, 1.0, 0.0), axis=0, keepdims=True)
    order = jnp.where(row_i.astype(f32) == rank, 1.0, 0.0)
    npts[...] = jnp.broadcast_to(jnp.sum(order * count, axis=1, keepdims=True), (lat, LANES))
    order = order.astype(bf16)
    in_slot = jnp.where(row_i == slot_ref[...], 1.0, 0.0).astype(bf16)
    place[...] = jnp.dot(order, in_slot, preferred_element_type=f32).astype(bf16)
    sources = four_ref.shape[0]
    for chunk in range(four_ref.shape[1] // MESSAGE):
        wide[...] = four_ref[:, pl.ds(chunk * MESSAGE, MESSAGE), :].astype(f32).reshape(wide.shape)
        for part in range(4):
            for r in range(2):
                halves = [wide[pl.ds(part * 4 + r * 2 + h, sources, stride=MESSAGE), :] for h in range(2)]
                held[part, pl.ds((chunk * 2 + r) * sources, sources), :] = jnp.concatenate(
                    halves, axis=1).astype(bf16)
    for part in range(4):
        moved = dot_nt(order, held[part])
        for t in range(tiles):
            live[part, t] = moved[:, t * LANES:(t + 1) * LANES]

    groups = SUBLANES // TOGETHER

    def multiply(t0, buf, far_count):
        count = 16 * far_count
        used, half = pl.ds(0, TOGETHER * count), LANES // 2
        even = dot_nt(left[buf][used, :waves], table[buf][:, :waves])
        odd = dot_nt(left[buf][used, waves:], table[buf][:, waves:])
        for l in range(TOGETHER):
            e = even[l * count:(l + 1) * count, l * half:(l + 1) * half]
            o = odd[l * count:(l + 1) * count, l * half:(l + 1) * half]
            rows[pl.ds(t0 + l, count, stride=lat + PAD), :] = jnp.concatenate([e - o, e + o], axis=1)

    def phases(i, far_count):
        middle_step = far_count // 2 - 1
        s0 = pl.multiple_of(jnp.minimum(i, lat // SUBLANES - 1) * SUBLANES, SUBLANES)
        points = npts[pl.ds(s0, SUBLANES), :]
        inverse = 1.0 / points
        for t in range(tiles):
            m = jnp.broadcast_to(wave_ref[:, t * LANES:(t + 1) * LANES].astype(f32), points.shape)
            weight = jnp.where(2.0 * m < points, jnp.where(m == 0.0, 1.0, 2.0), 0.0)
            half = turn(m, 2.0 * points, 0.5 * inverse)
            near = powers(times(half, half), 9)
            steps = powers(near[8], 5)
            for j, (c, s) in enumerate(steps):
                step_c[t, pl.ds(j * 8, 8), :] = c
                step_s[t, pl.ds(j * 8, 8), :] = s
            middle = times(half, steps[4])
            for j, w in enumerate(near[:8]):
                c, s = times(middle, w) if j else middle
                inner_c[t, pl.ds(j * 8, 8), :] = c
                inner_s[t, pl.ds(j * 8, 8), :] = s
            centre = times(times(steps[4], steps[4]), (half[0], -half[1]))
            outer = powers(turn(m * 128.0, points, inverse), 9)
            for j, (c, s) in enumerate(outer[:8]):
                outer_c[t, pl.ds(j * 8, 8), :] = c
                outer_s[t, pl.ds(j * 8, 8), :] = s
            far = powers(outer[8], far_count - middle_step)
            for j, (c, s) in enumerate(far[1:]):
                leap_c[t, pl.ds(j * 8, 8), :] = c
                leap_s[t, pl.ds(j * 8, 8), :] = s
            if middle_step:
                centre = times(centre, far[middle_step])
            for p in range(2):
                value = (
                    live[2 * p, t, pl.ds(s0, SUBLANES), :] * weight,
                    live[2 * p + 1, t, pl.ds(s0, SUBLANES), :] * weight,
                )
                r, im = times(value, centre)
                lead_r[t, pl.ds(p * 8, 8), :] = r
                lead_i[t, pl.ds(p * 8, 8), :] = im

    def block(i, carry, far_count, first):
        middle_step = far_count // 2 - 1
        s0 = pl.multiple_of(i * SUBLANES, SUBLANES)

        def make(l, buf):
            low, high = l % TOGETHER * (LANES // 2), l % TOGETHER * 16 * far_count

            def bcast(ref, t, row):
                return ref[t, pl.ds(row * 8 + l, 8, stride=0), :]

            def spread(ref, t):
                return ref[t, pl.ds(l, 8, stride=8), :]

            for t in range(tiles):
                ic, isn = spread(inner_c, t), spread(inner_s, t)
                cs, ss = [None] * 8, [None] * 8
                cs[4], ss[4] = ic, isn
                for j in range(1, 5):
                    wc, ws = bcast(step_c, t, j), bcast(step_s, t, j)
                    a, b, c, d = ic * wc, isn * ws, isn * wc, ic * ws
                    if j < 4:
                        cs[4 + j], ss[4 + j] = a - b, c + d
                    cs[4 - j], ss[4 - j] = a + b, c - d
                here = pl.ds(t * LANES, LANES)
                there = pl.ds(waves + t * LANES, LANES)
                for q in range(4):
                    table[buf][pl.ds(low + q * 16, 16), here] = jnp.concatenate(
                        [cs[2 * q], cs[2 * q + 1]], axis=0).astype(bf16)
                    table[buf][pl.ds(low + q * 16, 16), there] = jnp.concatenate(
                        [ss[2 * q], ss[2 * q + 1]], axis=0).astype(bf16)
                oc, os = spread(outer_c, t), spread(outer_s, t)
                parts = [[None] * far_count for _ in range(2)]
                for p in range(2):
                    parts[p][middle_step] = times(
                        (bcast(lead_r, t, p), bcast(lead_i, t, p)), (oc, os))
                for j in range(1, far_count - middle_step):
                    wc, ws = bcast(leap_c, t, j - 1), bcast(leap_s, t, j - 1)
                    for p in range(2):
                        r, im = parts[p][middle_step]
                        a, b, c, d = r * wc, im * ws, im * wc, r * ws
                        parts[p][middle_step + j] = (a - b, c + d)
                        if j <= middle_step:
                            parts[p][middle_step - j] = (a + b, c - d)
                for q in range(far_count):
                    for i, where in enumerate((here, there)):
                        left[buf][pl.ds(high + q * 16, 16), where] = jnp.concatenate(
                            [parts[0][q][i], parts[1][q][i]], axis=0).astype(bf16)

        for g in range(groups):
            for l in range(g * TOGETHER, (g + 1) * TOGETHER):
                make(l, g % 2)
            if g:
                multiply(s0 + (g - 1) * TOGETHER, (g - 1) % 2, far_count)
            else:
                before = jnp.where(i > first, s0 - TOGETHER, s0 + SUBLANES - TOGETHER)
                multiply(before, (groups - 1) % 2, far_count)
        phases(i + 1, far_count)
        return carry

    start = jnp.int32(0)
    for far_count in range(2, COARSE // 8 + 1, 2):
        if far_count == COARSE // 8:
            end = lat // SUBLANES
        else:
            fits = jnp.where(count <= far_count * 1024.0, 1.0, 0.0)
            end = jnp.sum(fits).astype(jnp.int32) // SUBLANES
        phases(start, far_count)
        lax.fori_loop(start, end, functools.partial(block, far_count=far_count, first=start), 0)

        @pl.when(end > start)
        def _(end=end, far_count=far_count):
            multiply(end * SUBLANES - TOGETHER, (groups - 1) % 2, far_count)

        start = end

    def longitude_of(shape):
        lane = lax.broadcasted_iota(jnp.int32, shape, 1)
        return jnp.where(lane < LANES // 2, lane + LANES // 2, LANES - 1 - lane)

    square = (LANES, LANES)
    small = jnp.where(lax.broadcasted_iota(jnp.int32, square, 0) == longitude_of(square), 1.0, 0.0).astype(bf16)
    npts[...] = npts[...] - longitude_of((lat, LANES)).astype(f32)

    def turned(p, a):
        at = (a // 8) * 16 + p * 8 + a % 8
        value = rows[pl.ds(pl.multiple_of(at * (lat + PAD), 8), lat), :]
        first = jnp.float32(a * LANES) if isinstance(a, int) else (a * LANES).astype(f32)
        return dot_nt(small, jnp.where(npts[...] > first, value, 0.0).astype(bf16)).astype(bf16)

    def placed(values):
        return jnp.dot(jnp.concatenate(values, axis=0), place[...], preferred_element_type=f32).astype(bf16)

    whole_blocks = lon // LANES

    def some(h, carry):
        for p in range(2):
            out_ref[p, pl.ds(pl.multiple_of(h * STEP * LANES, LANES), STEP * LANES), :] = placed(
                [turned(p, h * STEP + i) for i in range(STEP)])
        return carry

    lax.fori_loop(0, whole_blocks // STEP, some, 0)
    for p in range(2):
        for a in range(whole_blocks // STEP * STEP, blocks):
            size = min(LANES, lon - a * LANES)
            out_ref[p, a * LANES:a * LANES + size, :] = placed([turned(p, a)])[:size]


def zonal(four, wave_of_row, row_points, lat_slot, lon):
    waves, lat = wave_of_row.shape[0], lat_slot.shape[0]
    tiles = waves // LANES
    f32 = jnp.float32
    vmem = pl.BlockSpec(memory_space=pltpu.VMEM)

    left_shape = pltpu.VMEM((TOGETHER * 2 * COARSE, 2 * waves), jnp.bfloat16)
    table_shape = pltpu.VMEM((TOGETHER * LANES // 2, 2 * waves), jnp.bfloat16)

    def scratch(count):
        return pltpu.VMEM((tiles, count * 8, LANES), f32)

    return pl.pallas_call(
        zonal_kernel,
        out_shape=jax.ShapeDtypeStruct((2, lon, lat), jnp.bfloat16),
        in_specs=[vmem] * 4,
        out_specs=vmem,
        scratch_shapes=[
            pltpu.VMEM((4, tiles, lat, LANES), f32),
            pltpu.VMEM((lat, LANES), f32),
            pltpu.VMEM((lat, lat), jnp.bfloat16),
            pltpu.VMEM((four.shape[0] * MESSAGE, LANES), f32),
            pltpu.VMEM((4, waves, lat), jnp.bfloat16),
            scratch(8), scratch(8), scratch(5), scratch(5), scratch(8), scratch(8),
            scratch(COARSE // 16), scratch(COARSE // 16), scratch(2), scratch(2),
            left_shape, left_shape, table_shape, table_shape,
            pltpu.VMEM((2 * COARSE * (lat + PAD), LANES), f32),
        ],
        compiler_params=pltpu.CompilerParams(vmem_limit_bytes=48 * 1024 * 1024),
        cost_estimate=pl.CostEstimate(
            flops=2 * lat * 2 * COARSE * LANES * 2 * waves, bytes_accessed=7 << 20, transcendentals=0
        ),
    )(four, wave_of_row[None], row_points[None], lat_slot[None])


LON = 5136
MESH = pl.DeviceIdType.MESH


def spectral_kernel(
    spec_hbm, leg_ref, wave_ref, field_ref, recv_ref,
    spec_ref, legs, swap, lefts, mixed, outbox,
    spec_sem, own_sem, send_a, recv_a, send_f, recv_f, send_m, recv_m, keep_m,
):
    bf16, f32 = jnp.bfloat16, jnp.float32
    me, y = lax.axis_index("wave"), lax.axis_index("fld")
    peers, ring = lax.axis_size("wave"), lax.axis_size("fld")
    right, left = lax.rem(y + 1, ring), lax.rem(y + ring - 1, ring)
    rows_here, lats_here, degrees = leg_ref.shape
    chunks = rows_here // 2
    pairs = spec_ref.shape[0] * spec_ref.shape[2]

    def there(k):
        other = me + k
        return jnp.where(other >= peers, other - peers, other)

    barrier = pltpu.get_barrier_semaphore()

    def greet(k, carry):
        pl.semaphore_signal(barrier, inc=1, device_id=(there(k), y), device_id_type=MESH)
        return carry

    for side in (right, left):
        pl.semaphore_signal(barrier, inc=1, device_id=(me, side), device_id_type=MESH)
    lax.fori_loop(1, peers, greet, 0, unroll=9)

    def own():
        return pltpu.make_async_copy(leg_ref, legs.at[y], own_sem)

    def first(c, side):
        at = pl.ds(2 * c, 2)
        return pltpu.make_async_remote_copy(
            src_ref=leg_ref.at[at], dst_ref=legs.at[y, at],
            send_sem=send_a.at[side, c], recv_sem=recv_a.at[side, c],
            device_id=(me, (right, left)[side]), device_id_type=MESH)

    def second(c, side):
        block, at = (left, right)[side], pl.ds(2 * c + side, 1)
        return pltpu.make_async_remote_copy(
            src_ref=legs.at[block, at], dst_ref=legs.at[block, at],
            send_sem=send_f.at[side, c], recv_sem=recv_f.at[side, c],
            device_id=(me, (right, left)[side]), device_id_type=MESH)

    def rows_of(g):
        return pl.ds(BUNDLES[g][0] * MESSAGE, BUNDLES[g][1] * MESSAGE)

    def message(g, k):
        other = there(k)
        return pltpu.make_async_remote_copy(
            src_ref=outbox.at[other, rows_of(g)], dst_ref=recv_ref.at[me, rows_of(g)],
            send_sem=send_m.at[g], recv_sem=recv_m.at[g],
            device_id=(other, y), device_id_type=MESH)

    def all_messages(g):
        some = pl.ds(0, peers - 1)
        return pltpu.make_async_remote_copy(
            src_ref=outbox.at[some, rows_of(g)], dst_ref=recv_ref.at[some, rows_of(g)],
            send_sem=send_m.at[g], recv_sem=recv_m.at[g],
            device_id=(there(1), y), device_id_type=MESH)

    def kept(g):
        return pltpu.make_async_copy(outbox.at[me, rows_of(g)], recv_ref.at[me, rows_of(g)], keep_m.at[g])

    def spec_copy():
        return pltpu.make_async_copy(spec_hbm, spec_ref, spec_sem)

    spec_copy().start()
    own().start()

    row_i = lax.broadcasted_iota(jnp.int32, (pairs, pairs), 0)
    col_i = lax.broadcasted_iota(jnp.int32, (pairs, pairs), 1)
    eye = jnp.where(row_i == col_i, 1.0, 0.0).astype(bf16)
    twice_i = lax.broadcasted_iota(jnp.int32, (pairs // 2, pairs), 1)
    twice = jnp.where(
        lax.broadcasted_iota(jnp.int32, (pairs // 2, pairs), 0) == twice_i // 2, 1.0, 0.0).astype(bf16)
    fields = jnp.broadcast_to(field_ref[...].astype(f32), (8, pairs // 2)).astype(bf16)
    wanted = 2.0 * jnp.dot(fields, twice, preferred_element_type=f32)[0:1]
    wanted = wanted + (col_i[0:1] % 2).astype(f32)
    swap[...] = dot_nt(eye, jnp.where(row_i.astype(f32) == wanted, 1.0, 0.0).astype(bf16)).astype(bf16)

    def regroup(row, carry):
        lefts[row] = jnp.dot(
            swap[...], spec_ref[:, row].reshape(pairs, degrees), preferred_element_type=f32).astype(bf16)
        return carry

    spec_copy().wait()
    lax.fori_loop(0, 2, regroup, 0)
    own().wait()
    pl.semaphore_wait(barrier, peers + 1)
    for side in range(2):
        first(0, side).start()

    def pass_on(c):
        for side in range(2):
            first(c, side).wait_recv()
        for side in range(2):
            second(c, side).start()

        @pl.when(c < chunks - 1)
        def _():
            for side in range(2):
                first(c + 1, side).start()

    lax.fori_loop(2, EARLY, regroup, 0)
    pass_on(0)

    def step(c, carry):
        @pl.when(c < chunks - 1)
        def _():
            pass_on(c + 1)

        for side in range(2):
            second(c, side).wait_recv()
        degree = lax.broadcasted_iota(jnp.int32, (1, degrees), 1)
        for r in range(2):
            row = 2 * c + r
            values = jnp.concatenate([legs[g, row] for g in range(ring)], axis=0)
            keep = jnp.where(degree >= wave_ref[me * rows_here + row], 1.0, 0.0).astype(bf16)
            fourier = dot_nt(lefts[row], values * keep)
            for h in range(2):
                mixed[pl.ds(r * 2 + h, pairs, stride=4), :] = fourier[:, h * LANES:(h + 1) * LANES]
        outbox[:, pl.ds(pl.multiple_of(c * MESSAGE, MESSAGE), MESSAGE), :] = mixed[...].astype(bf16).reshape(
            peers, MESSAGE, LANES)
        return carry

    for g, (c0, size) in enumerate(BUNDLES):
        lax.fori_loop(c0, c0 + size, step, 0)
        kept(g).start()

        message(g, peers // 2).start()

        def post(k, carry, g=g):
            message(g, peers // 2 - k).start()
            message(g, peers // 2 + k).start()
            return carry

        lax.fori_loop(1, peers // 2, post, 0, unroll=4)
        row = EARLY + 2 * g
        lax.fori_loop(min(row, rows_here), min(row + 2, rows_here), regroup, 0)

    def finish(c, carry):
        for side in range(2):
            first(c, side).wait_send()
            second(c, side).wait_send()
        return carry

    lax.fori_loop(0, chunks, finish, 0)
    for g in range(len(BUNDLES)):
        kept(g).wait()
        all_messages(g).wait()


def spectral_part(spec, legendre, wave_of_row, field_slot, peers, ring):
    pairs, degrees = spec.shape[0] * spec.shape[2], spec.shape[3]
    rows_here = spec.shape[1]
    lats_here = legendre.shape[1]
    chunks = rows_here // 2
    bf16 = jnp.bfloat16
    vmem = pl.BlockSpec(memory_space=pltpu.VMEM)
    hbm = pl.BlockSpec(memory_space=pltpu.HBM)
    pairs_sem = pltpu.SemaphoreType.DMA((2, chunks))
    bundle_sem = pltpu.SemaphoreType.DMA((len(BUNDLES),))
    return pl.pallas_call(
        spectral_kernel,
        out_shape=jax.ShapeDtypeStruct((peers, chunks * MESSAGE, LANES), bf16),
        in_specs=[hbm, hbm, pl.BlockSpec(memory_space=pltpu.SMEM), vmem],
        out_specs=pl.BlockSpec(memory_space=pl.ANY),
        scratch_shapes=[
            pltpu.VMEM(spec.shape, bf16),
            pltpu.VMEM((ring, rows_here, lats_here, degrees), bf16),
            pltpu.VMEM((pairs, pairs), bf16),
            pltpu.VMEM((rows_here, pairs, degrees), bf16),
            pltpu.VMEM((peers * MESSAGE, LANES), jnp.float32),
            pltpu.VMEM((peers, chunks * MESSAGE, LANES), bf16),
            pltpu.SemaphoreType.DMA,
            pltpu.SemaphoreType.DMA,
            pairs_sem, pairs_sem, pairs_sem, pairs_sem, bundle_sem, bundle_sem, bundle_sem,
        ],
        compiler_params=pltpu.CompilerParams(
            collective_id=0, has_side_effects=True, vmem_limit_bytes=60 * 1024 * 1024),
        cost_estimate=pl.CostEstimate(
            flops=2 * rows_here * pairs * degrees * lats_here * ring, bytes_accessed=6 << 20, transcendentals=0),
    )(spec, legendre, wave_of_row, field_slot[None])


def local(spectral, legendre, wave_of_row, row_points, lat_slot, field_slot):
    rows_here, degree_count, _ = legendre.shape
    peers, ring = lax.axis_size("wave"), lax.axis_size("fld")
    spec = jnp.transpose(spectral[0], (0, 2, 1, 3))
    four = spectral_part(spec, jnp.transpose(legendre, (0, 2, 1)), wave_of_row, field_slot, peers, ring)
    waves = wave_of_row.reshape(peers, rows_here).T.reshape(-1)
    grid = zonal(four, waves, row_points, lat_slot, LON)
    return jnp.transpose(grid, (0, 2, 1))[None]


def solution(mesh):
    in_specs = (P("fld", None, None, "wave", None), P("wave", None, "fld"), P(), P(), P(), P())
    out_specs = P("fld", "wave", None, None)
    return jax.shard_map(local, mesh=mesh, in_specs=in_specs, out_specs=out_specs, check_vma=False)
```

```python
import functools
import math

import jax
import jax.numpy as jnp
from jax import lax
from jax.experimental import pallas as pl
from jax.experimental.pallas import tpu as pltpu
from jax.sharding import PartitionSpec as P

LANES = 128
SUBLANES = 8
STEP = 5
PAD = 8
TOGETHER = 2
MESSAGE = 16
EARLY = 6
BUNDLES = tuple((c, 1) for c in range(5))
COARSE = 48


def turn(product, points, inverse):
    residue = product - jnp.round(product * inverse) * points
    x = residue * inverse * (math.pi / 2)
    y = x * x
    s = x * (1.0 + y * (-1.0 / 6 + y * (1.0 / 120 + y * (-1.0 / 5040))))
    c = 1.0 + y * (-0.5 + y * (1.0 / 24 + y * (-1.0 / 720 + y * (1.0 / 40320))))
    for _ in range(2):
        c, s = 1.0 - 2.0 * s * s, 2.0 * s * c
    return c, s


def times(a, b):
    return a[0] * b[0] - a[1] * b[1], a[0] * b[1] + a[1] * b[0]


def powers(base, count):
    one = (jnp.ones_like(base[0]), jnp.zeros_like(base[0]))
    out = [one, base]
    for i in range(2, count):
        out.append(times(out[i // 2], out[i - i // 2]))
    return out[:count]


def dot_nt(a, b):
    return lax.dot_general(a, b, (((1,), (1,)), ((), ())), preferred_element_type=jnp.float32)


def zonal_kernel(
    four_ref, wave_ref, points_ref, slot_ref, out_ref,
    live, npts, place, wide, held, inner_c, inner_s, step_c, step_s, outer_c, outer_s, leap_c, leap_s, lead_r, lead_i, left_a, left_b, table_a, table_b, rows,
):
    lat = slot_ref.shape[1]
    waves = wave_ref.shape[1]
    tiles = waves // LANES
    lon = out_ref.shape[1]
    blocks = pl.cdiv(lon, LANES)
    bf16, f32 = jnp.bfloat16, jnp.float32
    left, table = (left_a, left_b), (table_a, table_b)

    row_i = lax.broadcasted_iota(jnp.int32, (lat, lat), 0)
    eye = jnp.where(row_i == lax.broadcasted_iota(jnp.int32, (lat, lat), 1), 1.0, 0.0)
    count = points_ref[...].astype(f32)
    count_down = jnp.sum(eye * count, axis=1, keepdims=True)
    rank = jnp.sum(jnp.where(count_down < count, 1.0, 0.0), axis=0, keepdims=True)
    order = jnp.where(row_i.astype(f32) == rank, 1.0, 0.0)
    npts[...] = jnp.broadcast_to(jnp.sum(order * count, axis=1, keepdims=True), (lat, LANES))
    order = order.astype(bf16)
    in_slot = jnp.where(row_i == slot_ref[...], 1.0, 0.0).astype(bf16)
    place[...] = jnp.dot(order, in_slot, preferred_element_type=f32).astype(bf16)
    sources = four_ref.shape[0]
    for chunk in range(four_ref.shape[1] // MESSAGE):
        wide[...] = four_ref[:, pl.ds(chunk * MESSAGE, MESSAGE), :].astype(f32).reshape(wide.shape)
        for part in range(4):
            for r in range(2):
                halves = [wide[pl.ds(part * 4 + r * 2 + h, sources, stride=MESSAGE), :] for h in range(2)]
                held[part, pl.ds((chunk * 2 + r) * sources, sources), :] = jnp.concatenate(
                    halves, axis=1).astype(bf16)
    for part in range(4):
        moved = dot_nt(order, held[part])
        for t in range(tiles):
            live[part, t] = moved[:, t * LANES:(t + 1) * LANES]

    groups = SUBLANES // TOGETHER

    def multiply(t0, buf, far_count):
        count = 16 * far_count
        used, half = pl.ds(0, TOGETHER * count), LANES // 2
        even = dot_nt(left[buf][used, :waves], table[buf][:, :waves])
        odd = dot_nt(left[buf][used, waves:], table[buf][:, waves:])
        for l in range(TOGETHER):
            e = even[l * count:(l + 1) * count, l * half:(l + 1) * half]
            o = odd[l * count:(l + 1) * count, l * half:(l + 1) * half]
            rows[pl.ds(t0 + l, count, stride=lat + PAD), :] = jnp.concatenate([e - o, e + o], axis=1)

    def phases(i, far_count):
        middle_step = (far_count - 1) // 2
        s0 = pl.multiple_of(jnp.minimum(i, lat // SUBLANES - 1) * SUBLANES, SUBLANES)
        points = npts[pl.ds(s0, SUBLANES), :]
        inverse = 1.0 / points
        for t in range(tiles):
            m = jnp.broadcast_to(wave_ref[:, t * LANES:(t + 1) * LANES].astype(f32), points.shape)
            weight = jnp.where(2.0 * m < points, jnp.where(m == 0.0, 1.0, 2.0), 0.0)
            half = turn(m, 2.0 * points, 0.5 * inverse)
            near = powers(times(half, half), 9)
            steps = powers(near[8], 5)
            for j, (c, s) in enumerate(steps):
                step_c[t, pl.ds(j * 8, 8), :] = c
                step_s[t, pl.ds(j * 8, 8), :] = s
            middle = times(half, steps[4])
            for j, w in enumerate(near[:8]):
                c, s = times(middle, w) if j else middle
                inner_c[t, pl.ds(j * 8, 8), :] = c
                inner_s[t, pl.ds(j * 8, 8), :] = s
            centre = times(times(steps[4], steps[4]), (half[0], -half[1]))
            outer = powers(turn(m * 128.0, points, inverse), 9)
            for j, (c, s) in enumerate(outer[:8]):
                outer_c[t, pl.ds(j * 8, 8), :] = c
                outer_s[t, pl.ds(j * 8, 8), :] = s
            far = powers(outer[8], far_count - middle_step)
            for j, (c, s) in enumerate(far[1:]):
                leap_c[t, pl.ds(j * 8, 8), :] = c
                leap_s[t, pl.ds(j * 8, 8), :] = s
            if middle_step:
                centre = times(centre, far[middle_step])
            for p in range(2):
                value = (
                    live[2 * p, t, pl.ds(s0, SUBLANES), :] * weight,
                    live[2 * p + 1, t, pl.ds(s0, SUBLANES), :] * weight,
                )
                r, im = times(value, centre)
                lead_r[t, pl.ds(p * 8, 8), :] = r
                lead_i[t, pl.ds(p * 8, 8), :] = im

    def block(i, carry, far_count, first):
        middle_step = (far_count - 1) // 2
        s0 = pl.multiple_of(i * SUBLANES, SUBLANES)

        def make(l, buf):
            low, high = l % TOGETHER * (LANES // 2), l % TOGETHER * 16 * far_count

            def bcast(ref, t, row):
                return ref[t, pl.ds(row * 8 + l, 8, stride=0), :]

            def spread(ref, t):
                return ref[t, pl.ds(l, 8, stride=8), :]

            for t in range(tiles):
                ic, isn = spread(inner_c, t), spread(inner_s, t)
                cs, ss = [None] * 8, [None] * 8
                cs[4], ss[4] = ic, isn
                for j in range(1, 5):
                    wc, ws = bcast(step_c, t, j), bcast(step_s, t, j)
                    a, b, c, d = ic * wc, isn * ws, isn * wc, ic * ws
                    if j < 4:
                        cs[4 + j], ss[4 + j] = a - b, c + d
                    cs[4 - j], ss[4 - j] = a + b, c - d
                here = pl.ds(t * LANES, LANES)
                there = pl.ds(waves + t * LANES, LANES)
                for q in range(4):
                    table[buf][pl.ds(low + q * 16, 16), here] = jnp.concatenate(
                        [cs[2 * q], cs[2 * q + 1]], axis=0).astype(bf16)
                    table[buf][pl.ds(low + q * 16, 16), there] = jnp.concatenate(
                        [ss[2 * q], ss[2 * q + 1]], axis=0).astype(bf16)
                oc, os = spread(outer_c, t), spread(outer_s, t)
                parts = [[None] * far_count for _ in range(2)]
                for p in range(2):
                    parts[p][middle_step] = times(
                        (bcast(lead_r, t, p), bcast(lead_i, t, p)), (oc, os))
                for j in range(1, far_count - middle_step):
                    wc, ws = bcast(leap_c, t, j - 1), bcast(leap_s, t, j - 1)
                    for p in range(2):
                        r, im = parts[p][middle_step]
                        a, b, c, d = r * wc, im * ws, im * wc, r * ws
                        parts[p][middle_step + j] = (a - b, c + d)
                        if j <= middle_step:
                            parts[p][middle_step - j] = (a + b, c - d)
                for q in range(far_count):
                    for i, where in enumerate((here, there)):
                        left[buf][pl.ds(high + q * 16, 16), where] = jnp.concatenate(
                            [parts[0][q][i], parts[1][q][i]], axis=0).astype(bf16)

        for g in range(groups):
            for l in range(g * TOGETHER, (g + 1) * TOGETHER):
                make(l, g % 2)
            if g:
                multiply(s0 + (g - 1) * TOGETHER, (g - 1) % 2, far_count)
            else:
                before = jnp.where(i > first, s0 - TOGETHER, s0 + SUBLANES - TOGETHER)
                multiply(before, (groups - 1) % 2, far_count)
        phases(i + 1, far_count)
        return carry

    start = jnp.int32(0)
    for far_count in range(1, COARSE // 8 + 1):
        if far_count == COARSE // 8:
            end = lat // SUBLANES
        else:
            fits = jnp.where(count <= far_count * 1024.0, 1.0, 0.0)
            end = jnp.sum(fits).astype(jnp.int32) // SUBLANES
        phases(start, far_count)
        lax.fori_loop(start, end, functools.partial(block, far_count=far_count, first=start), 0)

        @pl.when(end > start)
        def _(end=end, far_count=far_count):
            multiply(end * SUBLANES - TOGETHER, (groups - 1) % 2, far_count)

        start = end

    def longitude_of(shape):
        lane = lax.broadcasted_iota(jnp.int32, shape, 1)
        return jnp.where(lane < LANES // 2, lane + LANES // 2, LANES - 1 - lane)

    square = (LANES, LANES)
    small = jnp.where(lax.broadcasted_iota(jnp.int32, square, 0) == longitude_of(square), 1.0, 0.0).astype(bf16)
    npts[...] = npts[...] - longitude_of((lat, LANES)).astype(f32)

    def turned(p, a):
        at = (a // 8) * 16 + p * 8 + a % 8
        value = rows[pl.ds(pl.multiple_of(at * (lat + PAD), 8), lat), :]
        first = jnp.float32(a * LANES) if isinstance(a, int) else (a * LANES).astype(f32)
        return dot_nt(small, jnp.where(npts[...] > first, value, 0.0).astype(bf16)).astype(bf16)

    def placed(values):
        return jnp.dot(jnp.concatenate(values, axis=0), place[...], preferred_element_type=f32).astype(bf16)

    whole_blocks = lon // LANES

    def some(h, carry):
        for p in range(2):
            out_ref[p, pl.ds(pl.multiple_of(h * STEP * LANES, LANES), STEP * LANES), :] = placed(
                [turned(p, h * STEP + i) for i in range(STEP)])
        return carry

    lax.fori_loop(0, whole_blocks // STEP, some, 0)
    for p in range(2):
        for a in range(whole_blocks // STEP * STEP, blocks):
            size = min(LANES, lon - a * LANES)
            out_ref[p, a * LANES:a * LANES + size, :] = placed([turned(p, a)])[:size]


def zonal(four, wave_of_row, row_points, lat_slot, lon):
    waves, lat = wave_of_row.shape[0], lat_slot.shape[0]
    tiles = waves // LANES
    f32 = jnp.float32
    vmem = pl.BlockSpec(memory_space=pltpu.VMEM)

    left_shape = pltpu.VMEM((TOGETHER * 2 * COARSE, 2 * waves), jnp.bfloat16)
    table_shape = pltpu.VMEM((TOGETHER * LANES // 2, 2 * waves), jnp.bfloat16)

    def scratch(count):
        return pltpu.VMEM((tiles, count * 8, LANES), f32)

    return pl.pallas_call(
        zonal_kernel,
        out_shape=jax.ShapeDtypeStruct((2, lon, lat), jnp.bfloat16),
        in_specs=[vmem] * 4,
        out_specs=vmem,
        scratch_shapes=[
            pltpu.VMEM((4, tiles, lat, LANES), f32),
            pltpu.VMEM((lat, LANES), f32),
            pltpu.VMEM((lat, lat), jnp.bfloat16),
            pltpu.VMEM((four.shape[0] * MESSAGE, LANES), f32),
            pltpu.VMEM((4, waves, lat), jnp.bfloat16),
            scratch(8), scratch(8), scratch(5), scratch(5), scratch(8), scratch(8),
            scratch(COARSE // 16), scratch(COARSE // 16), scratch(2), scratch(2),
            left_shape, left_shape, table_shape, table_shape,
            pltpu.VMEM((2 * COARSE * (lat + PAD), LANES), f32),
        ],
        compiler_params=pltpu.CompilerParams(vmem_limit_bytes=48 * 1024 * 1024),
        cost_estimate=pl.CostEstimate(
            flops=2 * lat * 2 * COARSE * LANES * 2 * waves, bytes_accessed=7 << 20, transcendentals=0
        ),
    )(four, wave_of_row[None], row_points[None], lat_slot[None])


LON = 5136
MESH = pl.DeviceIdType.MESH


def spectral_kernel(
    spec_hbm, leg_ref, wave_ref, field_ref, recv_ref,
    spec_ref, legs, swap, lefts, mixed, outbox,
    spec_sem, own_sem, send_a, recv_a, send_f, recv_f, send_m, recv_m, keep_m,
):
    bf16, f32 = jnp.bfloat16, jnp.float32
    me, y = lax.axis_index("wave"), lax.axis_index("fld")
    peers, ring = lax.axis_size("wave"), lax.axis_size("fld")
    right, left = lax.rem(y + 1, ring), lax.rem(y + ring - 1, ring)
    rows_here, lats_here, degrees = leg_ref.shape
    chunks = rows_here // 2
    pairs = spec_ref.shape[0] * spec_ref.shape[2]

    def there(k):
        other = me + k
        return jnp.where(other >= peers, other - peers, other)

    barrier = pltpu.get_barrier_semaphore()

    def greet(k, carry):
        pl.semaphore_signal(barrier, inc=1, device_id=(there(k), y), device_id_type=MESH)
        return carry

    for side in (right, left):
        pl.semaphore_signal(barrier, inc=1, device_id=(me, side), device_id_type=MESH)
    lax.fori_loop(1, peers, greet, 0, unroll=9)

    def own():
        return pltpu.make_async_copy(leg_ref, legs.at[y], own_sem)

    def first(c, side):
        at = pl.ds(2 * c, 2)
        return pltpu.make_async_remote_copy(
            src_ref=leg_ref.at[at], dst_ref=legs.at[y, at],
            send_sem=send_a.at[side, c], recv_sem=recv_a.at[side, c],
            device_id=(me, (right, left)[side]), device_id_type=MESH)

    def second(c, side):
        block, at = (left, right)[side], pl.ds(2 * c + side, 1)
        return pltpu.make_async_remote_copy(
            src_ref=legs.at[block, at], dst_ref=legs.at[block, at],
            send_sem=send_f.at[side, c], recv_sem=recv_f.at[side, c],
            device_id=(me, (right, left)[side]), device_id_type=MESH)

    def rows_of(g):
        return pl.ds(BUNDLES[g][0] * MESSAGE, BUNDLES[g][1] * MESSAGE)

    def message(g, k):
        other = there(k)
        return pltpu.make_async_remote_copy(
            src_ref=outbox.at[other, rows_of(g)], dst_ref=recv_ref.at[me, rows_of(g)],
            send_sem=send_m.at[g], recv_sem=recv_m.at[g],
            device_id=(other, y), device_id_type=MESH)

    def all_messages(g):
        some = pl.ds(0, peers - 1)
        return pltpu.make_async_remote_copy(
            src_ref=outbox.at[some, rows_of(g)], dst_ref=recv_ref.at[some, rows_of(g)],
            send_sem=send_m.at[g], recv_sem=recv_m.at[g],
            device_id=(there(1), y), device_id_type=MESH)

    def kept(g):
        return pltpu.make_async_copy(outbox.at[me, rows_of(g)], recv_ref.at[me, rows_of(g)], keep_m.at[g])

    def spec_copy():
        return pltpu.make_async_copy(spec_hbm, spec_ref, spec_sem)

    spec_copy().start()
    own().start()

    row_i = lax.broadcasted_iota(jnp.int32, (pairs, pairs), 0)
    col_i = lax.broadcasted_iota(jnp.int32, (pairs, pairs), 1)
    eye = jnp.where(row_i == col_i, 1.0, 0.0).astype(bf16)
    twice_i = lax.broadcasted_iota(jnp.int32, (pairs // 2, pairs), 1)
    twice = jnp.where(
        lax.broadcasted_iota(jnp.int32, (pairs // 2, pairs), 0) == twice_i // 2, 1.0, 0.0).astype(bf16)
    fields = jnp.broadcast_to(field_ref[...].astype(f32), (8, pairs // 2)).astype(bf16)
    wanted = 2.0 * jnp.dot(fields, twice, preferred_element_type=f32)[0:1]
    wanted = wanted + (col_i[0:1] % 2).astype(f32)
    swap[...] = dot_nt(eye, jnp.where(row_i.astype(f32) == wanted, 1.0, 0.0).astype(bf16)).astype(bf16)

    def regroup(row, carry):
        lefts[row] = jnp.dot(
            swap[...], spec_ref[:, row].reshape(pairs, degrees), preferred_element_type=f32).astype(bf16)
        return carry

    spec_copy().wait()
    lax.fori_loop(0, 2, regroup, 0)
    own().wait()
    pl.semaphore_wait(barrier, peers + 1)
    for c in range(2):
        for side in range(2):
            first(c, side).start()

    def pass_on(c):
        for side in range(2):
            first(c, side).wait_recv()
        for side in range(2):
            second(c, side).start()

        @pl.when(c < chunks - 2)
        def _():
            for side in range(2):
                first(c + 2, side).start()

    lax.fori_loop(2, EARLY, regroup, 0)
    pass_on(0)

    def step(c, carry):
        @pl.when(c < chunks - 1)
        def _():
            pass_on(c + 1)

        for side in range(2):
            second(c, side).wait_recv()
        degree = lax.broadcasted_iota(jnp.int32, (1, degrees), 1)
        for r in range(2):
            row = 2 * c + r
            values = jnp.concatenate([legs[g, row] for g in range(ring)], axis=0)
            keep = jnp.where(degree >= wave_ref[me * rows_here + row], 1.0, 0.0).astype(bf16)
            fourier = dot_nt(lefts[row], values * keep)
            for h in range(2):
                mixed[pl.ds(r * 2 + h, pairs, stride=4), :] = fourier[:, h * LANES:(h + 1) * LANES]
        outbox[:, pl.ds(pl.multiple_of(c * MESSAGE, MESSAGE), MESSAGE), :] = mixed[...].astype(bf16).reshape(
            peers, MESSAGE, LANES)
        return carry

    for g, (c0, size) in enumerate(BUNDLES):
        lax.fori_loop(c0, c0 + size, step, 0)
        kept(g).start()

        message(g, peers // 2).start()

        def post(k, carry, g=g):
            message(g, peers // 2 - k).start()
            message(g, peers // 2 + k).start()
            return carry

        lax.fori_loop(1, peers // 2, post, 0, unroll=4)
        row = EARLY + 2 * g
        lax.fori_loop(min(row, rows_here), min(row + 2, rows_here), regroup, 0)

    def finish(c, carry):
        for side in range(2):
            first(c, side).wait_send()
            second(c, side).wait_send()
        return carry

    lax.fori_loop(0, chunks, finish, 0)
    for g in range(len(BUNDLES)):
        kept(g).wait()
        all_messages(g).wait()


def spectral_part(spec, legendre, wave_of_row, field_slot, peers, ring):
    pairs, degrees = spec.shape[0] * spec.shape[2], spec.shape[3]
    rows_here = spec.shape[1]
    lats_here = legendre.shape[1]
    chunks = rows_here // 2
    bf16 = jnp.bfloat16
    vmem = pl.BlockSpec(memory_space=pltpu.VMEM)
    hbm = pl.BlockSpec(memory_space=pltpu.HBM)
    pairs_sem = pltpu.SemaphoreType.DMA((2, chunks))
    bundle_sem = pltpu.SemaphoreType.DMA((len(BUNDLES),))
    return pl.pallas_call(
        spectral_kernel,
        out_shape=jax.ShapeDtypeStruct((peers, chunks * MESSAGE, LANES), bf16),
        in_specs=[hbm, hbm, pl.BlockSpec(memory_space=pltpu.SMEM), vmem],
        out_specs=pl.BlockSpec(memory_space=pl.ANY),
        scratch_shapes=[
            pltpu.VMEM(spec.shape, bf16),
            pltpu.VMEM((ring, rows_here, lats_here, degrees), bf16),
            pltpu.VMEM((pairs, pairs), bf16),
            pltpu.VMEM((rows_here, pairs, degrees), bf16),
            pltpu.VMEM((peers * MESSAGE, LANES), jnp.float32),
            pltpu.VMEM((peers, chunks * MESSAGE, LANES), bf16),
            pltpu.SemaphoreType.DMA,
            pltpu.SemaphoreType.DMA,
            pairs_sem, pairs_sem, pairs_sem, pairs_sem, bundle_sem, bundle_sem, bundle_sem,
        ],
        compiler_params=pltpu.CompilerParams(
            collective_id=0, has_side_effects=True, vmem_limit_bytes=60 * 1024 * 1024),
        cost_estimate=pl.CostEstimate(
            flops=2 * rows_here * pairs * degrees * lats_here * ring, bytes_accessed=6 << 20, transcendentals=0),
    )(spec, legendre, wave_of_row, field_slot[None])


def local(spectral, legendre, wave_of_row, row_points, lat_slot, field_slot):
    rows_here, degree_count, _ = legendre.shape
    peers, ring = lax.axis_size("wave"), lax.axis_size("fld")
    spec = jnp.transpose(spectral[0], (0, 2, 1, 3))
    four = spectral_part(spec, jnp.transpose(legendre, (0, 2, 1)), wave_of_row, field_slot, peers, ring)
    waves = wave_of_row.reshape(peers, rows_here).T.reshape(-1)
    grid = zonal(four, waves, row_points, lat_slot, LON)
    return jnp.transpose(grid, (0, 2, 1))[None]


def solution(mesh):
    in_specs = (P("fld", None, None, "wave", None), P("wave", None, "fld"), P(), P(), P(), P())
    out_specs = P("fld", "wave", None, None)
    return jax.shard_map(local, mesh=mesh, in_specs=in_specs, out_specs=out_specs, check_vma=False)
```
